32 devices in a mesh: seq: 8 (over z, y), head: 4 (over x, core).
Axes of the slice: x: 2, y: 2, z: 4, core: 2. Of those that a mesh axis runs over, the one named last changes fastest.
Arguments:
- hidden: bfloat16 [1, 4096, 1024], P(None, 'seq'), may hold values from -6 to 6
- prescale: float32 [1024], replicated, may hold values from 0.5 to 1.5
- gating: bfloat16 [1024, 2048], P(None, 'head'), may hold values from -0.1875 to 0.1875
- feature: bfloat16 [1024, 2048], P(None, 'head'), may hold values from -0.1875 to 0.1875
- selective: bfloat16 [1024, 256], replicated, may hold values from -0.1875 to 0.1875
- timestep: bfloat16 [1024, 32], P(None, 'head'), may hold values from -0.1875 to 0.1875
- filters: float32 [4, 2048], P(None, 'head'), may hold values from -3 to 3
- statefilters: float32 [4, 256], replicated, may hold values from -3 to 3
- offsets: float32 [2048], P('head'), may hold values from -0.5 to 0.5
- stateoffsets: float32 [256], replicated, may hold values from -0.5 to 0.5
- stepbias: float32 [32], P('head'), may hold values from -6 to -2
- decaylog: float32 [32], P('head'), may hold values from -9 to 0
- skipgain: float32 [32], P('head'), may hold values from 0.5 to 1.5
- postscale: float32 [2048], P('head'), may hold values from 0.5 to 1.5
- projection: bfloat16 [1024, 2048], P(None, 'head'), may hold values from -0.125 to 0.125
- cotangent: bfloat16 [1, 4096, 1024], P(None, 'seq', 'head'), may hold values from -6 to 6
Outputs:
- output: bfloat16 [1, 4096, 1024], P(None, 'seq', 'head')
- hidden_grad: float32 [1, 4096, 1024], P(None, 'seq')
- prescale_grad: float32 [1024], P('seq')
- gating_grad: float32 [1024, 2048], P('seq', 'head')
- feature_grad: float32 [1024, 2048], P('seq', 'head')
- selective_grad: float32 [1024, 256], P('seq')
- timestep_grad: float32 [1024, 32], P('seq', 'head')
- filters_grad: float32 [4, 2048], P(None, 'head')
- statefilters_grad: float32 [4, 256], replicated
- offsets_grad: float32 [2048], P('head')
- stateoffsets_grad: float32 [256], replicated
- stepbias_grad: float32 [32], P('head')
- decaylog_grad: float32 [32], P('head')
- skipgain_grad: float32 [32], P('head')
- postscale_grad: float32 [2048], P('head')
- projection_grad: float32 [1024, 2048], P('seq', 'head')
The draws below stay inside these ranges and needn't reach their ends.
All inputs are finite; a program needn't handle non-finite values.
Results may differ from the reference program's by a relative error of at most 0.029.
Values may be sent and summed in bfloat16 or wider, within the bound.
A program may use at most 192 MiB of HBM per device.

```python
import jax
import jax.numpy as jnp
from jax import lax

D = 1024
HEADS = 32
HEAD_DIM = 64
STATE = 128
TAPS = 4
GROUP = 256
SEQS = 1
DI = 2048
LENGTH = 4096


def shard_levels(own_key, dims, cuts, smallest, top_value):
    gain = 1.0
    for position, parts in cuts:
        draws = jax.random.uniform(jax.random.fold_in(jax.random.fold_in(own_key, 6), position), (parts,), jnp.float32, smallest / len(cuts), top_value / len(cuts))
        gain = gain * jnp.repeat(jnp.exp(draws), dims[position] // parts).reshape((-1,) + (1,) * (len(dims) - 1 - position))
    return gain


def centred(key, dims, scale, reach, shards=(), kind=jnp.bfloat16):
    drawn = scale * jax.random.normal(key, dims, jnp.float32)
    if shards:
        drawn = drawn * shard_levels(key, dims, shards, -0.22, 0.18)
    return jnp.clip(drawn, -reach, reach).astype(kind)


def setup_inputs(seed: int = 0) -> dict:
    arg_keys = jax.random.split(jax.random.key(seed), 17)
    return {
        "hidden": centred(arg_keys[0], (SEQS, LENGTH, D), 1.0, 6.0, ((1, 8),)),
        "prescale": jnp.clip(1.0 + 0.1 * jax.random.normal(arg_keys[1], (D,), jnp.float32), 0.5, 1.5),
        "gating": centred(arg_keys[2], (D, DI), D ** -0.5, 0.1875, ((1, 4),)),
        "feature": centred(arg_keys[3], (D, DI), D ** -0.5, 0.1875, ((1, 4),)),
        "selective": centred(arg_keys[4], (D, 2 * STATE), D ** -0.5, 0.1875),
        "timestep": centred(arg_keys[5], (D, HEADS), D ** -0.5, 0.1875, ((1, 4),)),
        "filters": centred(arg_keys[6], (TAPS, DI), TAPS ** -0.5, 3.0, ((1, 4),), jnp.float32),
        "statefilters": centred(arg_keys[7], (TAPS, 2 * STATE), TAPS ** -0.5, 3.0, (), jnp.float32),
        "offsets": jnp.clip(jax.random.uniform(arg_keys[8], (DI,), jnp.float32, -0.5, 0.5) * shard_levels(arg_keys[8], (DI,), ((0, 4),), -0.4, 0.0), -0.5, 0.5),
        "stateoffsets": jnp.clip(jax.random.uniform(arg_keys[9], (2 * STATE,), jnp.float32, -0.5, 0.5), -0.5, 0.5),
        "stepbias": jnp.clip(-6.0 + 4.0 * jax.random.uniform(arg_keys[10], (HEADS,), jnp.float32) ** shard_levels(arg_keys[10], (HEADS,), ((0, 4),), -0.2, 0.2), -6.0, -2.0),
        "decaylog": jnp.clip(-9.0 + 9.0 * jax.random.uniform(arg_keys[11], (HEADS,), jnp.float32) ** shard_levels(arg_keys[11], (HEADS,), ((0, 4),), -0.2, 0.2), -9.0, 0.0),
        "skipgain": jnp.clip(0.5 + 1.0 * jax.random.uniform(arg_keys[12], (HEADS,), jnp.float32) ** shard_levels(arg_keys[12], (HEADS,), ((0, 4),), -0.2, 0.2), 0.5, 1.5),
        "postscale": jnp.clip(1.0 + 0.1 * jax.random.normal(arg_keys[13], (DI,), jnp.float32), 0.5, 1.5),
        "projection": centred(arg_keys[14], (D, DI), DI ** -0.5, 0.125, ((1, 4),)),
        "cotangent": centred(arg_keys[15], (SEQS, LENGTH, D), 1.0, 6.0, ((1, 8), (2, 4))),
    }


eps_norm = 1e-05
exact = lax.Precision.HIGHEST

@jax.custom_vjp
def low(v):
    return lax.optimization_barrier(v.astype(jnp.bfloat16)).astype(jnp.float32)

@jax.custom_vjp
def low_back(v):
    return v

def low_keep(v):
    return (low(v), None)

def low_pass(kept, grad):
    return (grad,)

def back_keep(v):
    return (v, None)

def back_low(kept, grad):
    return (low(grad),)
low.defvjp(low_keep, low_pass)
low_back.defvjp(back_keep, back_low)

def group_step(memory, pieces, rates, skipping):
    inputs, deltas, writers, readers = pieces
    blocklen = inputs.shape[0]
    causal = lax.broadcasted_iota(jnp.int32, (blocklen, blocklen), 0) >= lax.broadcasted_iota(jnp.int32, (blocklen, blocklen), 1)
    decays = deltas * rates[None, :]
    running = jnp.dot(causal.astype(jnp.float32), decays, precision=exact)
    across = running.T
    spread = across[:, :, None] - across[:, None, :]
    inside = jnp.where(causal[None], jnp.exp(jnp.where(causal[None], spread, 0.0)), 0.0)
    scores = jnp.dot(readers, writers.T, precision=exact)
    mixing = inside * scores[None] * deltas.T[:, None, :]
    direct = jnp.einsum('hij,jhp->ihp', mixing, inputs, precision=exact)
    carried = jnp.exp(running)[:, :, None] * jnp.einsum('in,hpn->ihp', readers, memory, precision=exact)
    result = direct + carried + skipping[None, :, None] * inputs
    finale = running[-1]
    toward = jnp.exp(finale[None, :] - running) * deltas
    incoming = jnp.einsum('jh,jhp,jn->hpn', toward, inputs, writers, precision=exact)
    return (jnp.exp(finale)[:, None, None] * memory + incoming, result)

def causal_filter(values, weights, offset):
    tapcount = weights.shape[0]
    rowcount = values.shape[0]
    padded = jnp.concatenate([jnp.zeros((tapcount - 1, values.shape[1]), jnp.float32), values], axis=0)
    summed = offset[None, :] + weights[0][None, :] * padded[0:rowcount]
    for tapindex in range(1, tapcount):
        summed = summed + weights[tapindex][None, :] * padded[tapindex:tapindex + rowcount]
    return summed

def layer(hidden, prescale, gating, feature, selective, timestep, filters, statefilters, offsets, stateoffsets, stepbias, decaylog, skipgain, postscale, projection):
    rowscale = lax.rsqrt(lax.optimization_barrier(jnp.mean(hidden * hidden, axis=1, keepdims=True)) + eps_norm)
    normed = low(hidden * rowscale * prescale[None, :])
    gate_raw = low_back(jnp.dot(normed, gating, precision=exact))
    inner_pre = low_back(low(jnp.dot(normed, feature, precision=exact)))
    state_pre = low(jnp.dot(normed, selective, precision=exact))
    step_raw = low_back(jnp.dot(normed, timestep, precision=exact))
    inner_act = low(jax.nn.silu(causal_filter(inner_pre, filters, offsets)))
    state_act = low(jax.nn.silu(causal_filter(state_pre, statefilters, stateoffsets)))
    deltas = jax.nn.softplus(step_raw + stepbias[None, :])
    rates = -jnp.exp(decaylog)
    blocks = LENGTH // GROUP
    pieces = (inner_act.reshape(blocks, GROUP, HEADS, HEAD_DIM), deltas.reshape(blocks, GROUP, HEADS), state_act[:, :STATE].reshape(blocks, GROUP, STATE), state_act[:, STATE:].reshape(blocks, GROUP, STATE))

    def advance(memory, piece):
        return group_step(memory, piece, rates, skipgain)
    start = jnp.zeros((HEADS, HEAD_DIM, STATE), jnp.float32)
    final_memory, outputs = lax.scan(jax.checkpoint(advance), start, pieces)
    mixed = outputs.reshape(LENGTH, HEADS * HEAD_DIM)
    gated = mixed * jax.nn.silu(gate_raw)
    gated_scale = lax.rsqrt(lax.optimization_barrier(jnp.mean(gated * gated, axis=1, keepdims=True)) + eps_norm)
    normed_out = low(gated * gated_scale * postscale[None, :])
    return hidden + jnp.dot(normed_out, projection.T, precision=exact)

def reference(hidden, prescale, gating, feature, selective, timestep, filters, statefilters, offsets, stateoffsets, stepbias, decaylog, skipgain, postscale, projection, cotangent):
    params = (prescale, gating.astype(jnp.float32), feature.astype(jnp.float32), selective.astype(jnp.float32), timestep.astype(jnp.float32), filters, statefilters, offsets, stateoffsets, stepbias, decaylog, skipgain, postscale, projection.astype(jnp.float32))

    def one_sequence(totals, couple):
        sequence, incoming = couple
        result, pullback = jax.vjp(layer, sequence.astype(jnp.float32), *params)
        grads = pullback(incoming.astype(jnp.float32))
        summed = tuple((former + latter for former, latter in zip(totals, grads[1:])))
        return (summed, (result.astype(jnp.bfloat16), grads[0]))
    initial = tuple((jnp.zeros(member.shape, jnp.float32) for member in params))
    totals, (outputs, hidden_grad) = lax.scan(one_sequence, initial, (hidden, cotangent))
    return (outputs, hidden_grad, totals[0], totals[1], totals[2], totals[3], totals[4], totals[5], totals[6], totals[7], totals[8], totals[9], totals[10], totals[11], totals[12], totals[13])
```

```python
import functools

import jax
import jax.numpy as jnp
from jax import lax
from jax.experimental import pallas as pl
from jax.experimental.pallas import tpu as pltpu
from jax.sharding import PartitionSpec as P

GROUP = 256
VMEM_LIMIT = 48 * 2**20


eps_norm = 1e-05
exact = lax.Precision.HIGHEST


def passed_along(shard, axis, by):
    count = lax.axis_size(axis)
    pairs = [(i, i + by) for i in range(count) if 0 <= i + by < count]
    return lax.ppermute(shard, axis, pairs)


def greet(axis, n):
    me = lax.axis_index(axis)
    barrier = pltpu.get_barrier_semaphore()
    for k in range(1, n):
        pl.semaphore_signal(
            barrier,
            inc=1,
            device_id={axis: lax.rem(me + k, n)},
            device_id_type=pl.DeviceIdType.MESH,
        )
    pl.semaphore_wait(barrier, n - 1)
    return me


def push(source, target, sends, arrivals, k, axis, n):
    copy = pltpu.make_async_remote_copy(
        src_ref=source,
        dst_ref=target,
        send_sem=sends.at[k],
        recv_sem=arrivals.at[k],
        device_id={axis: lax.rem(lax.axis_index(axis) + k, n)},
        device_id_type=pl.DeviceIdType.MESH,
    )
    copy.start()
    return copy


def gather_kernel(axis, n, x_ref, o_ref, sends, arrivals):
    me = greet(axis, n)
    copies = [push(x_ref, o_ref.at[me], sends, arrivals, k, axis, n) for k in range(1, n)]
    o_ref[me] = x_ref[...]
    for copy in copies:
        copy.wait()


def gathered(x, axis, ident):
    n = lax.axis_size(axis)
    if n > 8:
        return lax.all_gather(x, axis)
    return pl.pallas_call(
        functools.partial(gather_kernel, axis, n),
        out_shape=jax.ShapeDtypeStruct((n, *x.shape), x.dtype),
        in_specs=[pl.BlockSpec(memory_space=pltpu.VMEM)],
        out_specs=pl.BlockSpec(memory_space=pltpu.VMEM),
        scratch_shapes=[pltpu.SemaphoreType.DMA((n,)), pltpu.SemaphoreType.DMA((n,))],
        compiler_params=pltpu.CompilerParams(
            collective_id=ident, has_side_effects=True, vmem_limit_bytes=VMEM_LIMIT
        ),
    )(x)


def allsum_kernel(axis, n, x_ref, o_ref, landed, send1, recv1, send2, recv2):
    me = greet(axis, n)
    firsts = [
        push(x_ref.at[lax.rem(me + k, n)], landed.at[k], send1, recv1, k, axis, n)
        for k in range(1, n)
    ]
    for copy in firsts:
        copy.wait()
    total = x_ref[me].astype(jnp.float32)
    for k in range(1, n):
        total = total + landed[k].astype(jnp.float32)
    o_ref[me] = total.astype(o_ref.dtype)
    seconds = [push(o_ref.at[me], o_ref.at[me], send2, recv2, k, axis, n) for k in range(1, n)]
    for copy in seconds:
        copy.wait()


def summed(x, axis, ident):
    n = lax.axis_size(axis)
    rows, columns = x.shape
    if n > 8 or rows % (16 * n):
        return lax.psum(x, axis)
    piece = (n, rows // n, columns)
    return pl.pallas_call(
        functools.partial(allsum_kernel, axis, n),
        out_shape=jax.ShapeDtypeStruct(piece, x.dtype),
        in_specs=[pl.BlockSpec(memory_space=pltpu.VMEM)],
        out_specs=pl.BlockSpec(memory_space=pltpu.VMEM),
        scratch_shapes=[pltpu.VMEM(piece, x.dtype)] + [pltpu.SemaphoreType.DMA((n,))] * 4,
        compiler_params=pltpu.CompilerParams(
            collective_id=ident, has_side_effects=True, vmem_limit_bytes=VMEM_LIMIT
        ),
    )(x.reshape(piece)).reshape(rows, columns)


def relay_kernel(axis, n, backwards, s_ref, d_ref, o_ref, s_in, d_in, out, sends, recvs):
    me = greet(axis, n)
    firsts = []
    for k in range(1, n):
        peer = lax.rem(me + k, n)
        firsts.append(push(d_ref.at[peer], d_in.at[me], sends.at[0], recvs.at[0], k, axis, n))
        firsts.append(push(s_ref.at[peer], s_in.at[me], sends.at[1], recvs.at[1], k, axis, n))
    d_in[me] = d_ref[me]
    s_in[me] = s_ref[me]
    for copy in firsts:
        copy.wait()
    total = jnp.zeros(s_ref.shape[1:], jnp.float32)
    for p in range(n - 1, -1, -1) if backwards else range(n):
        out[p] = total.astype(out.dtype)
        total = d_in[p][0:1, :] * total + s_in[p].astype(jnp.float32)
    o_ref[me] = out[me]
    seconds = [
        push(out.at[lax.rem(me + k, n)], o_ref.at[me], sends.at[2], recvs.at[2], k, axis, n)
        for k in range(1, n)
    ]
    for copy in seconds:
        copy.wait()


def relayed(states, decays, axis, backwards, ident):
    n = lax.axis_size(axis)
    heads, rows, columns = states.shape
    if heads != n:
        place = lax.axis_index(axis)
        allstates = lax.all_gather(states.astype(jnp.bfloat16), axis)
        alldecays = lax.all_gather(decays, axis)

        def hop(k, total):
            source = n - 1 - k if backwards else k
            reached = source > place if backwards else source < place
            new = alldecays[source][:, None, None] * total + allstates[source].astype(jnp.float32)
            return jnp.where(reached, new, total)

        return lax.fori_loop(0, n, hop, jnp.zeros(states.shape, jnp.float32)).astype(jnp.bfloat16)
    return pl.pallas_call(
        functools.partial(relay_kernel, axis, n, backwards),
        out_shape=jax.ShapeDtypeStruct(states.shape, jnp.bfloat16),
        in_specs=[pl.BlockSpec(memory_space=pltpu.VMEM)] * 2,
        out_specs=pl.BlockSpec(memory_space=pltpu.VMEM),
        scratch_shapes=[
            pltpu.VMEM(states.shape, jnp.bfloat16),
            pltpu.VMEM((n, 8, columns), jnp.float32),
            pltpu.VMEM(states.shape, jnp.bfloat16),
            pltpu.SemaphoreType.DMA((3, n)),
            pltpu.SemaphoreType.DMA((3, n)),
        ],
        compiler_params=pltpu.CompilerParams(
            collective_id=ident, has_side_effects=True, vmem_limit_bytes=VMEM_LIMIT
        ),
    )(
        states.astype(jnp.bfloat16),
        jnp.broadcast_to(decays[:, None, None], (n, 8, columns)),
    )


def states_kernel(heads, v_ref, w_ref, b_ref, o_ref):
    size = v_ref.shape[1] // heads
    columns = b_ref[...]
    for h in range(heads):
        span = slice(h * size, (h + 1) * size)
        weighted = v_ref[:, span].astype(jnp.float32) * w_ref[:, h : h + 1]
        o_ref[span, :] = contract_first(weighted.astype(jnp.bfloat16), columns).astype(o_ref.dtype)


def weighted_states(values, weights, columns):
    heads = weights.shape[1]
    return pl.pallas_call(
        functools.partial(states_kernel, heads),
        out_shape=jax.ShapeDtypeStruct((values.shape[1], columns.shape[1]), jnp.bfloat16),
        compiler_params=pltpu.CompilerParams(vmem_limit_bytes=VMEM_LIMIT),
    )(values, weights, columns)


def decay_part(cum_ref, across_ref, h, top, below):
    rows = lax.broadcasted_iota(jnp.int32, (below - top, below), 0) + top
    columns = lax.broadcasted_iota(jnp.int32, (below - top, below), 1)
    spread = cum_ref[top:below, h : h + 1] - across_ref[h : h + 1, 0:below]
    return jnp.exp(jnp.where(rows >= columns, spread, -1e30))


def ssm_kernel(heads, x_ref, w_ref, r_ref, dt_ref, cum_ref, across_ref, s_ref, skip_ref, y_ref):
    tokens = x_ref.shape[0]
    size = x_ref.shape[1] // heads
    chunk = min(GROUP, tokens)
    for top in range(0, tokens, chunk):
        below = top + chunk
        scores = contract_last(r_ref[top:below, :], w_ref[0:below, :])
        for h in range(heads):
            span = slice(h * size, (h + 1) * size)
            inputs = x_ref[0:below, span].astype(jnp.float32)
            mixing = (scores * decay_part(cum_ref, across_ref, h, top, below)).astype(jnp.bfloat16)
            driven = (inputs * dt_ref[0:below, h : h + 1]).astype(jnp.bfloat16)
            result = jnp.dot(mixing, driven, preferred_element_type=jnp.float32)
            carried = contract_last(r_ref[top:below, :], s_ref[span, :])
            result = result + jnp.exp(cum_ref[top:below, h : h + 1]) * carried
            y_ref[top:below, span] = result + skip_ref[0:1, h : h + 1] * inputs[top:below]


def ssm_forward(inputs, writers, readers, deltas, cum, across, entering, skipping):
    heads = deltas.shape[1]
    return pl.pallas_call(
        functools.partial(ssm_kernel, heads),
        out_shape=jax.ShapeDtypeStruct(inputs.shape, jnp.float32),
        compiler_params=pltpu.CompilerParams(vmem_limit_bytes=VMEM_LIMIT),
    )(inputs, writers, readers, deltas, cum, across, entering, skipping)


def back_kernel(
    heads,
    x_ref,
    w_ref,
    r_ref,
    dt_ref,
    cum_ref,
    across_ref,
    s_ref,
    skip_ref,
    y_ref,
    dy_ref,
    l_ref,
    dx_ref,
    dw_ref,
    dr_ref,
    col_ref,
    mix_ref,
    back_ref,
):
    tokens = x_ref.shape[0]
    size = x_ref.shape[1] // heads
    chunk = min(GROUP, tokens)
    f32, b16 = jnp.float32, jnp.bfloat16
    for top in range(0, tokens, chunk):
        below = top + chunk
        scores = contract_last(r_ref[top:below, :], w_ref[0:below, :])
        for h in range(heads):
            span = slice(h * size, (h + 1) * size)
            decay = decay_part(cum_ref, across_ref, h, top, below)
            mixing = (scores * decay).astype(b16)
            driven = (x_ref[0:below, span].astype(f32) * dt_ref[0:below, h : h + 1]).astype(b16)
            grads = dy_ref[top:below, span].astype(b16)
            share = contract_last(grads, driven) * decay
            if h == 0:
                mix_ref[:, 0:below] = share
            else:
                mix_ref[:, 0:below] += share
            back = contract_first(mixing, grads)
            if top:
                back_ref[0:top, span] += back[0:top]
            back_ref[top:below, span] = back[top:below]
        mixed = mix_ref[:, 0:below].astype(b16)
        dr_ref[top:below, :] = jnp.dot(mixed, w_ref[0:below, :], preferred_element_type=f32)
        written = contract_first(mixed, r_ref[top:below, :])
        if top:
            dw_ref[0:top, :] += written[0:top]
        dw_ref[top:below, :] = written[top:below]
    for h in range(heads):
        span = slice(h * size, (h + 1) * size)
        step = dt_ref[:, h : h + 1]
        run = cum_ref[:, h : h + 1]
        skipping = skip_ref[0:1, h : h + 1]
        inputs = x_ref[:, span].astype(f32)
        grads = dy_ref[:, span]
        rounded = grads.astype(b16).astype(f32)
        driven = (inputs * step).astype(b16).astype(f32)
        left = jnp.exp(run[tokens - 1 : tokens, :] - run)
        later = left * contract_last(w_ref[...], l_ref[span, :])
        inner = back_ref[:, span]
        both = inner + later
        dx_ref[:, span] = step * both + skipping * grads
        dr_ref[...] += jnp.dot(
            (jnp.exp(run) * grads).astype(b16), s_ref[span, :], preferred_element_type=f32
        )
        dw_ref[...] += jnp.dot(
            (left * driven).astype(b16), l_ref[span, :], preferred_element_type=f32
        )
        alone = y_ref[:, span] - skipping * inputs
        col_ref[:, h : h + 1] = jnp.sum(rounded * alone - driven * both, axis=1, keepdims=True)
        col_ref[:, heads + h : heads + h + 1] = jnp.sum(inputs * both, axis=1, keepdims=True)
        at = 2 * heads + h
        col_ref[:, at : at + 1] = jnp.sum(driven * later, axis=1, keepdims=True)
        at = 3 * heads + h
        col_ref[:, at : at + 1] = jnp.sum(inputs * grads, axis=1, keepdims=True)


def ssm_backward(
    inputs, writers, readers, deltas, cum, across, entering, skipping, mixed, mixed_grad, leaving
):
    tokens, heads = deltas.shape
    chunk = min(GROUP, tokens)
    return pl.pallas_call(
        functools.partial(back_kernel, heads),
        out_shape=(
            jax.ShapeDtypeStruct(inputs.shape, jnp.float32),
            jax.ShapeDtypeStruct(writers.shape, jnp.float32),
            jax.ShapeDtypeStruct(readers.shape, jnp.float32),
            jax.ShapeDtypeStruct((tokens, 4 * heads), jnp.float32),
        ),
        scratch_shapes=[
            pltpu.VMEM((chunk, tokens), jnp.float32),
            pltpu.VMEM(inputs.shape, jnp.float32),
        ],
        compiler_params=pltpu.CompilerParams(vmem_limit_bytes=VMEM_LIMIT),
    )(
        inputs,
        writers,
        readers,
        deltas,
        cum,
        across,
        entering,
        skipping,
        mixed,
        mixed_grad,
        leaving,
    )


def swish_slope(values):
    sigma = jax.nn.sigmoid(values)
    return sigma * (1.0 + values * (1.0 - sigma))


def contract_last(former, latter):
    return lax.dot_general(
        former, latter, (((1,), (1,)), ((), ())), preferred_element_type=jnp.float32
    )


def contract_first(former, latter):
    return lax.dot_general(
        former, latter, (((0,), (0,)), ((), ())), preferred_element_type=jnp.float32
    )


def local(
    hidden,
    prescale,
    gating,
    feature,
    selective,
    timestep,
    filters,
    statefilters,
    offsets,
    stateoffsets,
    stepbias,
    decaylog,
    skipgain,
    postscale,
    projection,
    cotangent,
):
    seqcount, tokens, modelwidth = hidden.shape
    heads_here = stepbias.shape[0]
    inner_here = gating.shape[1]
    headsize = inner_here // heads_here
    statesize = selective.shape[1] // 2
    tapcount = filters.shape[0]
    rowcount = seqcount * tokens
    inner_all = inner_here * lax.axis_size("head")
    flat_in = hidden.reshape(rowcount, modelwidth).astype(jnp.float32)
    rowscale = lax.rsqrt(jnp.mean(flat_in * flat_in, axis=1, keepdims=True) + eps_norm)
    normed = (flat_in * rowscale * prescale[None, :]).astype(jnp.bfloat16)
    gate_raw = jnp.dot(normed, gating, preferred_element_type=jnp.float32)
    inner_pre = jnp.dot(normed, feature, preferred_element_type=jnp.float32).astype(jnp.bfloat16)
    state_pre = jnp.dot(normed, selective, preferred_element_type=jnp.float32).astype(jnp.bfloat16)
    step_raw = jnp.dot(normed, timestep, preferred_element_type=jnp.float32)
    channels = jnp.concatenate([inner_pre, state_pre], axis=1).reshape(
        seqcount, tokens, inner_here + 2 * statesize
    )
    edge_in = passed_along(channels[:, tokens - tapcount + 1 :, :], "seq", 1)
    padded = jnp.concatenate([edge_in, channels], axis=1).astype(jnp.float32)
    kernel = jnp.concatenate([filters, statefilters], axis=1)
    shifts = jnp.concatenate([offsets, stateoffsets], axis=0)
    filtered = shifts[None, None, :] + kernel[0][None, None, :] * padded[:, 0:tokens]
    for tapindex in range(1, tapcount):
        filtered = (
            filtered + kernel[tapindex][None, None, :] * padded[:, tapindex : tapindex + tokens]
        )
    activity = jax.nn.silu(filtered).astype(jnp.bfloat16)[0]
    inner_x = activity[:, :inner_here]
    writers = activity[:, inner_here : inner_here + statesize]
    readers = activity[:, inner_here + statesize :]
    step_sum = step_raw + stepbias[None, :]
    deltas = jax.nn.softplus(step_sum)
    rates = -jnp.exp(decaylog)
    causal = (
        lax.broadcasted_iota(jnp.int32, (tokens, tokens), 0)
        >= lax.broadcasted_iota(jnp.int32, (tokens, tokens), 1)
    ).astype(jnp.float32)
    running = jnp.dot(causal, deltas * rates[None, :], precision=exact)
    across = running.T
    finale = running[-1]
    overall = jnp.exp(finale)
    skipping = skipgain[None, :]
    local_end = weighted_states(inner_x, jnp.exp(finale[None, :] - running) * deltas, writers)
    state_shape = (heads_here, headsize, statesize)
    entering = relayed(local_end.reshape(state_shape), overall, "seq", False, 0)
    flat_entering = entering.reshape(inner_here, statesize)
    mixed = ssm_forward(
        inner_x, writers, readers, deltas, running, across, flat_entering, skipping
    )
    upstream = lax.all_gather(cotangent, "head", axis=2, tiled=True).reshape(rowcount, modelwidth)
    normed_out_grad = jnp.dot(upstream, projection, preferred_element_type=jnp.float32)
    scaled_grad = normed_out_grad * postscale[None, :]
    gate_act = jax.nn.silu(gate_raw)
    gated = mixed * gate_act
    sums = jnp.concatenate(
        [jnp.sum(gated * gated, axis=1), jnp.sum(scaled_grad * gated, axis=1)]
    ).reshape(-1, 128)
    sums = jnp.sum(gathered(sums, "head", 1), axis=0).reshape(2, rowcount)
    row_terms = sums[1]
    gated_scale = lax.rsqrt(sums[0][:, None] / inner_all + eps_norm)
    normed_out = (gated * gated_scale * postscale[None, :]).astype(jnp.bfloat16)
    partial_out = contract_last(normed_out, projection)
    out_share = lax.psum_scatter(
        partial_out.astype(jnp.bfloat16), "head", scatter_dimension=1, tiled=True
    ).astype(jnp.float32)
    quarter = out_share.shape[1]
    residual = lax.dynamic_slice_in_dim(flat_in, lax.axis_index("head") * quarter, quarter, 1)
    output = (residual + out_share).astype(jnp.bfloat16).reshape(seqcount, tokens, quarter)
    projection_grad = contract_first(upstream, normed_out)
    postscale_grad = jnp.sum(normed_out_grad * gated * gated_scale, axis=0)
    gated_grad = gated_scale * scaled_grad - gated * gated_scale**3 * row_terms[:, None] / inner_all
    mixed_grad = gated_grad * gate_act
    gate_grad = (gated_grad * mixed * swish_slope(gate_raw)).astype(jnp.bfloat16)
    carry_entering = weighted_states(mixed_grad, jnp.exp(running), readers)
    leaving = relayed(carry_entering.reshape(state_shape), overall, "seq", True, 2)
    local_inner, writers_grad, readers_grad, terms = ssm_backward(
        inner_x,
        writers,
        readers,
        deltas,
        running,
        across,
        flat_entering,
        skipping,
        mixed,
        mixed_grad,
        leaving.reshape(inner_here, statesize),
    )
    at_end = jnp.sum(terms[:, 2 * heads_here : 3 * heads_here], axis=0) + overall * jnp.sum(
        entering.astype(jnp.float32) * leaving.astype(jnp.float32), axis=(1, 2)
    )
    decays_grad = at_end[None, :] + lax.dot_general(
        causal, terms[:, :heads_here], (((0,), (0,)), ((), ())), precision=exact
    )
    deltas_grad = terms[:, heads_here : 2 * heads_here] + rates[None, :] * decays_grad
    skipgain_grad = jnp.sum(terms[:, 3 * heads_here :], axis=0)
    decaylog_grad = jnp.sum(deltas * decays_grad, axis=0) * rates
    step_full = deltas_grad * jax.nn.sigmoid(step_sum)
    stepbias_grad = jnp.sum(step_full, axis=0)
    step_grad = step_full.astype(jnp.bfloat16)
    state_act_grad = jnp.concatenate([writers_grad, readers_grad], axis=1)
    state_act_grad = summed(state_act_grad.astype(jnp.bfloat16), "head", 3).astype(jnp.float32)
    local_inner = local_inner[None]
    state_act_grad = state_act_grad[None]
    act_grad = jnp.concatenate([local_inner, state_act_grad], axis=2)
    filtered_grad = act_grad * swish_slope(filtered)
    kernel_grad = jnp.stack(
        [
            jnp.sum(padded[:, tapindex : tapindex + tokens] * filtered_grad, axis=(0, 1))
            for tapindex in range(tapcount)
        ]
    )
    shifts_grad = jnp.sum(filtered_grad, axis=(0, 1))
    padded_grad = jnp.pad(
        kernel[0][None, None, :] * filtered_grad, ((0, 0), (0, tapcount - 1), (0, 0))
    )
    for tapindex in range(1, tapcount):
        padded_grad = padded_grad + jnp.pad(
            kernel[tapindex][None, None, :] * filtered_grad,
            ((0, 0), (tapindex, tapcount - 1 - tapindex), (0, 0)),
        )
    edge_back = passed_along(padded_grad[:, : tapcount - 1], "seq", -1)
    channel_grad = padded_grad[:, tapcount - 1 :] + jnp.pad(
        edge_back, ((0, 0), (tokens - tapcount + 1, 0), (0, 0))
    )
    inner_pre_grad = (
        channel_grad[:, :, :inner_here].reshape(rowcount, inner_here).astype(jnp.bfloat16)
    )
    state_pre_grad = channel_grad[:, :, inner_here:].reshape(rowcount, 2 * statesize)
    partial_in = (
        contract_last(gate_grad, gating)
        + contract_last(inner_pre_grad, feature)
        + contract_last(step_grad, timestep)
    )
    state_term = lax.dot_general(
        state_pre_grad, selective.astype(jnp.float32), (((1,), (1,)), ((), ())), precision=exact
    )
    mine = 2 * statesize // lax.axis_size("head")
    state_share = lax.dynamic_slice_in_dim(
        state_pre_grad, lax.axis_index("head") * mine, mine, 1
    )
    selective_grad = lax.dot_general(
        normed.astype(jnp.float32), state_share, (((0,), (0,)), ((), ())), precision=exact
    )
    statefilters_grad = kernel_grad[:, inner_here:]
    stateoffsets_grad = shifts_grad[inner_here:]
    normed_grad = summed(partial_in.astype(jnp.bfloat16), "head", 4).astype(jnp.float32)
    normed_grad = normed_grad + state_term
    gating_grad = contract_first(normed, gate_grad)
    feature_grad = contract_first(normed, inner_pre_grad)
    timestep_grad = contract_first(normed, step_grad)
    prescale_grad = jnp.sum(normed_grad * flat_in * rowscale, axis=0)
    scaled_in = normed_grad * prescale[None, :]
    row_in = jnp.sum(scaled_in * flat_in, axis=1, keepdims=True)
    hidden_grad = (
        upstream.astype(jnp.float32)
        + rowscale * scaled_in
        - flat_in * rowscale**3 * row_in / modelwidth
    )
    hidden_grad = hidden_grad.reshape(seqcount, tokens, modelwidth)
    gating_grad, feature_grad, projection_grad = (
        lax.psum_scatter(
            part.astype(jnp.bfloat16), "seq", scatter_dimension=0, tiled=True
        ).astype(jnp.float32)
        for part in (gating_grad, feature_grad, projection_grad)
    )
    narrow = jnp.concatenate(
        [selective_grad, timestep_grad, prescale_grad[:, None]], axis=1
    ).astype(jnp.bfloat16)
    narrow = jnp.pad(narrow, ((0, 0), (0, -narrow.shape[1] % 128)))
    narrow = lax.psum_scatter(narrow, "seq", scatter_dimension=0, tiled=True)
    timestep_grad = narrow[:, mine : mine + heads_here].astype(jnp.float32)
    prescale_grad = narrow[:, mine + heads_here].astype(jnp.float32)
    around = gathered(narrow, "head", 5)[:, :, :mine]
    selective_grad = (
        around.transpose(1, 0, 2).reshape(narrow.shape[0], 2 * statesize).astype(jnp.float32)
    )
    small = (
        kernel_grad[:, :inner_here],
        statefilters_grad,
        shifts_grad[:inner_here],
        stateoffsets_grad,
        postscale_grad,
        stepbias_grad,
        decaylog_grad,
        skipgain_grad,
    )
    packed = jnp.concatenate([part.reshape(-1) for part in small])
    packed = jnp.pad(packed, (0, -packed.shape[0] % 1024)).reshape(-1, 128)
    packed = jnp.sum(gathered(packed, "seq", 6), axis=0).reshape(-1)
    at, finished = 0, []
    for part in small:
        finished.append(packed[at : at + part.size].reshape(part.shape))
        at += part.size
    (
        filters_grad,
        statefilters_grad,
        offsets_grad,
        stateoffsets_grad,
        postscale_grad,
        stepbias_grad,
        decaylog_grad,
        skipgain_grad,
    ) = finished
    return (
        output,
        hidden_grad,
        prescale_grad,
        gating_grad,
        feature_grad,
        selective_grad,
        timestep_grad,
        filters_grad,
        statefilters_grad,
        offsets_grad,
        stateoffsets_grad,
        stepbias_grad,
        decaylog_grad,
        skipgain_grad,
        postscale_grad,
        projection_grad,
    )


def solution(mesh):
    placed = (
        P(None, "seq", None),
        P(),
        P(None, "head"),
        P(None, "head"),
        P(),
        P(None, "head"),
        P(None, "head"),
        P(),
        P("head"),
        P(),
        P("head"),
        P("head"),
        P("head"),
        P("head"),
        P(None, "head"),
        P(None, "seq", "head"),
    )
    return jax.shard_map(
        local,
        mesh=mesh,
        in_specs=placed,
        out_specs=(
            P(None, "seq", "head"),
            P(None, "seq", None),
            P("seq"),
            P("seq", "head"),
            P("seq", "head"),
            P("seq", None),
            P("seq", "head"),
            P(None, "head"),
            P(),
            P("head"),
            P(),
            P("head"),
            P("head"),
            P("head"),
            P("head"),
            P("seq", "head"),
        ),
        check_vma=False,
    )
```

```python
import functools

import jax
import jax.numpy as jnp
from jax import lax
from jax.experimental import pallas as pl
from jax.experimental.pallas import tpu as pltpu
from jax.sharding import PartitionSpec as P

GROUP = 256
VMEM_LIMIT = 48 * 2**20


eps_norm = 1e-05
exact = lax.Precision.HIGHEST


def passed_along(shard, axis, by):
    count = lax.axis_size(axis)
    pairs = [(i, i + by) for i in range(count) if 0 <= i + by < count]
    return lax.ppermute(shard, axis, pairs)


def greet(axis, n):
    me = lax.axis_index(axis)
    barrier = pltpu.get_barrier_semaphore()
    for k in range(1, n):
        pl.semaphore_signal(
            barrier,
            inc=1,
            device_id={axis: lax.rem(me + k, n)},
            device_id_type=pl.DeviceIdType.MESH,
        )
    pl.semaphore_wait(barrier, n - 1)
    return me


def push(source, target, sends, arrivals, k, axis, n):
    copy = pltpu.make_async_remote_copy(
        src_ref=source,
        dst_ref=target,
        send_sem=sends.at[k],
        recv_sem=arrivals.at[k],
        device_id={axis: lax.rem(lax.axis_index(axis) + k, n)},
        device_id_type=pl.DeviceIdType.MESH,
    )
    copy.start()
    return copy


def gather_kernel(axis, n, x_ref, o_ref, sends, arrivals):
    me = greet(axis, n)
    copies = [push(x_ref, o_ref.at[me], sends, arrivals, k, axis, n) for k in range(1, n)]
    o_ref[me] = x_ref[...]
    for copy in copies:
        copy.wait()


def gathered(x, axis, ident):
    n = lax.axis_size(axis)
    if n > 8:
        return lax.all_gather(x, axis)
    return pl.pallas_call(
        functools.partial(gather_kernel, axis, n),
        out_shape=jax.ShapeDtypeStruct((n, *x.shape), x.dtype),
        in_specs=[pl.BlockSpec(memory_space=pltpu.VMEM)],
        out_specs=pl.BlockSpec(memory_space=pltpu.VMEM),
        scratch_shapes=[pltpu.SemaphoreType.DMA((n,)), pltpu.SemaphoreType.DMA((n,))],
        compiler_params=pltpu.CompilerParams(
            collective_id=ident, has_side_effects=True, vmem_limit_bytes=VMEM_LIMIT
        ),
    )(x)


def allsum_kernel(axis, n, x_ref, o_ref, landed, send1, recv1, send2, recv2):
    me = greet(axis, n)
    firsts = [
        push(x_ref.at[lax.rem(me + k, n)], landed.at[k], send1, recv1, k, axis, n)
        for k in range(1, n)
    ]
    for copy in firsts:
        copy.wait()
    total = x_ref[me].astype(jnp.float32)
    for k in range(1, n):
        total = total + landed[k].astype(jnp.float32)
    o_ref[me] = total.astype(o_ref.dtype)
    seconds = [push(o_ref.at[me], o_ref.at[me], send2, recv2, k, axis, n) for k in range(1, n)]
    for copy in seconds:
        copy.wait()


def summed(x, axis, ident):
    n = lax.axis_size(axis)
    rows, columns = x.shape
    if n > 8 or rows % (16 * n):
        return lax.psum(x, axis)
    piece = (n, rows // n, columns)
    return pl.pallas_call(
        functools.partial(allsum_kernel, axis, n),
        out_shape=jax.ShapeDtypeStruct(piece, x.dtype),
        in_specs=[pl.BlockSpec(memory_space=pltpu.VMEM)],
        out_specs=pl.BlockSpec(memory_space=pltpu.VMEM),
        scratch_shapes=[pltpu.VMEM(piece, x.dtype)] + [pltpu.SemaphoreType.DMA((n,))] * 4,
        compiler_params=pltpu.CompilerParams(
            collective_id=ident, has_side_effects=True, vmem_limit_bytes=VMEM_LIMIT
        ),
    )(x.reshape(piece)).reshape(rows, columns)


def remote(source, target, send, arrival, axis, index):
    copy = pltpu.make_async_remote_copy(
        src_ref=source,
        dst_ref=target,
        send_sem=send,
        recv_sem=arrival,
        device_id={axis: index},
        device_id_type=pl.DeviceIdType.MESH,
    )
    copy.start()
    return copy


def finish_kernel(heads, n, count, *refs):
    t_ref, x_refs = refs[0], refs[1 : 1 + count]
    refs = refs[1 + count :]
    sum_ref, o_refs = refs[0], refs[1 : 1 + count]
    refs = refs[1 + count :]
    landed, near, parts, far = (
        refs[0],
        refs[1 : 1 + count],
        refs[1 + count : 1 + 2 * count],
        refs[1 + 2 * count : 1 + 3 * count],
    )
    hs1, hr1, hs2, hr2, s1, r1, s2, r2 = refs[1 + 3 * count :]
    across, along = lax.axis_index("head"), lax.axis_index("seq")
    half = n // 2
    row, side = along // 2, along % 2
    partner = 2 * row + 1 - side
    barrier = pltpu.get_barrier_semaphore()
    greeted = [("head", lax.rem(across + k, heads)) for k in range(1, heads)]
    greeted.append(("seq", partner))
    greeted += [("seq", 2 * lax.rem(row + k, half) + side) for k in range(1, half)]
    for axis, index in greeted:
        pl.semaphore_signal(
            barrier, inc=1, device_id={axis: index}, device_id_type=pl.DeviceIdType.MESH
        )
    pl.semaphore_wait(barrier, len(greeted))
    first = []
    for c in range(count):
        first.append(
            [
                remote(
                    x_refs[c].at[2 * j + 1 - side],
                    near[c].at[j],
                    s1.at[c, j],
                    r1.at[c, j],
                    "seq",
                    partner,
                )
                for j in range(half)
            ]
        )
    turn = []
    for k in range(1, heads):
        peer = lax.rem(across + k, heads)
        turn.append(remote(t_ref.at[peer], landed.at[k], hs1.at[k], hr1.at[k], "head", peer))

    def second(c):
        for copy in first[c]:
            copy.wait()
        for j in range(half):
            total = x_refs[c][2 * j + side].astype(jnp.float32) + near[c][j].astype(jnp.float32)
            parts[c][j] = total.astype(jnp.bfloat16)
        copies = []
        for k in range(1, half):
            peer = lax.rem(row + k, half)
            copies.append(
                remote(
                    parts[c].at[peer],
                    far[c].at[k],
                    s2.at[c, k],
                    r2.at[c, k],
                    "seq",
                    2 * peer + side,
                )
            )
        return copies

    later = [second(0)]
    for copy in turn:
        copy.wait()
    total = t_ref[across].astype(jnp.float32)
    for k in range(1, heads):
        total = total + landed[k].astype(jnp.float32)
    sum_ref[across] = total.astype(jnp.bfloat16)
    back = []
    for k in range(1, heads):
        peer = lax.rem(across + k, heads)
        back.append(
            remote(sum_ref.at[across], sum_ref.at[across], hs2.at[k], hr2.at[k], "head", peer)
        )
    for c in range(1, count):
        later.append(second(c))
    for c in range(count):
        for copy in later[c]:
            copy.wait()
        total = parts[c][row].astype(jnp.float32)
        for k in range(1, half):
            total = total + far[c][k].astype(jnp.float32)
        o_refs[c][...] = total
    for copy in back:
        copy.wait()


def finished_sums(terms, grads, ident):
    heads, n = lax.axis_size("head"), lax.axis_size("seq")
    rows, columns = terms.shape
    if n > 8 or n % 2 or rows % (16 * heads) or grads[0].shape[0] % (16 * n):
        shares = [
            lax.psum_scatter(part, "seq", scatter_dimension=0, tiled=True).astype(jnp.float32)
            for part in grads
        ]
        return summed(terms, "head", ident), shares
    count, half = len(grads), n // 2
    piece = (heads, rows // heads, columns)
    blocks = [(part.shape[0] // n, part.shape[1]) for part in grads]
    vmem = pl.BlockSpec(memory_space=pltpu.VMEM)
    landing = [pltpu.VMEM((half, *block), jnp.bfloat16) for block in blocks]
    total, *shares = pl.pallas_call(
        functools.partial(finish_kernel, heads, n, count),
        out_shape=(
            jax.ShapeDtypeStruct(piece, jnp.bfloat16),
            *(jax.ShapeDtypeStruct(block, jnp.float32) for block in blocks),
        ),
        in_specs=[vmem] * (1 + count),
        out_specs=(vmem,) * (1 + count),
        scratch_shapes=[pltpu.VMEM(piece, jnp.bfloat16)]
        + landing * 3
        + [pltpu.SemaphoreType.DMA((heads,))] * 4
        + [pltpu.SemaphoreType.DMA((count, half))] * 4,
        compiler_params=pltpu.CompilerParams(
            collective_id=ident, has_side_effects=True, vmem_limit_bytes=VMEM_LIMIT
        ),
    )(
        terms.reshape(piece),
        *(part.reshape(n, *block) for part, block in zip(grads, blocks)),
    )
    return total.reshape(rows, columns), shares


def relay_kernel(axis, n, backwards, s_ref, d_ref, o_ref, s_in, d_in, out, sends, recvs):
    me = greet(axis, n)
    firsts = []
    for k in range(1, n):
        peer = lax.rem(me + k, n)
        firsts.append(push(d_ref.at[peer], d_in.at[me], sends.at[0], recvs.at[0], k, axis, n))
        firsts.append(push(s_ref.at[peer], s_in.at[me], sends.at[1], recvs.at[1], k, axis, n))
    d_in[me] = d_ref[me]
    s_in[me] = s_ref[me]
    for copy in firsts:
        copy.wait()
    total = jnp.zeros(s_ref.shape[1:], jnp.float32)
    for p in range(n - 1, -1, -1) if backwards else range(n):
        out[p] = total.astype(out.dtype)
        total = d_in[p][0:1, :] * total + s_in[p].astype(jnp.float32)
    o_ref[me] = out[me]
    seconds = [
        push(out.at[lax.rem(me + k, n)], o_ref.at[me], sends.at[2], recvs.at[2], k, axis, n)
        for k in range(1, n)
    ]
    for copy in seconds:
        copy.wait()


def relayed(states, decays, axis, backwards, ident):
    n = lax.axis_size(axis)
    heads, rows, columns = states.shape
    if heads != n:
        place = lax.axis_index(axis)
        allstates = lax.all_gather(states.astype(jnp.bfloat16), axis)
        alldecays = lax.all_gather(decays, axis)

        def hop(k, total):
            source = n - 1 - k if backwards else k
            reached = source > place if backwards else source < place
            new = alldecays[source][:, None, None] * total + allstates[source].astype(jnp.float32)
            return jnp.where(reached, new, total)

        return lax.fori_loop(0, n, hop, jnp.zeros(states.shape, jnp.float32)).astype(jnp.bfloat16)
    return pl.pallas_call(
        functools.partial(relay_kernel, axis, n, backwards),
        out_shape=jax.ShapeDtypeStruct(states.shape, jnp.bfloat16),
        in_specs=[pl.BlockSpec(memory_space=pltpu.VMEM)] * 2,
        out_specs=pl.BlockSpec(memory_space=pltpu.VMEM),
        scratch_shapes=[
            pltpu.VMEM(states.shape, jnp.bfloat16),
            pltpu.VMEM((n, 8, columns), jnp.float32),
            pltpu.VMEM(states.shape, jnp.bfloat16),
            pltpu.SemaphoreType.DMA((3, n)),
            pltpu.SemaphoreType.DMA((3, n)),
        ],
        compiler_params=pltpu.CompilerParams(
            collective_id=ident, has_side_effects=True, vmem_limit_bytes=VMEM_LIMIT
        ),
    )(
        states.astype(jnp.bfloat16),
        jnp.broadcast_to(decays[:, None, None], (n, 8, columns)),
    )


def states_kernel(heads, v_ref, w_ref, b_ref, o_ref):
    size = v_ref.shape[1] // heads
    columns = b_ref[...]
    for h in range(heads):
        span = slice(h * size, (h + 1) * size)
        weighted = v_ref[:, span].astype(jnp.float32) * w_ref[:, h : h + 1]
        o_ref[span, :] = contract_first(weighted.astype(jnp.bfloat16), columns).astype(o_ref.dtype)


def weighted_states(values, weights, columns):
    heads = weights.shape[1]
    return pl.pallas_call(
        functools.partial(states_kernel, heads),
        out_shape=jax.ShapeDtypeStruct((values.shape[1], columns.shape[1]), jnp.bfloat16),
        compiler_params=pltpu.CompilerParams(vmem_limit_bytes=VMEM_LIMIT),
    )(values, weights, columns)


def decay_part(cum_ref, across_ref, h, top, below):
    rows = lax.broadcasted_iota(jnp.int32, (below - top, below), 0) + top
    columns = lax.broadcasted_iota(jnp.int32, (below - top, below), 1)
    spread = cum_ref[top:below, h : h + 1] - across_ref[h : h + 1, 0:below]
    return jnp.exp(jnp.where(rows >= columns, spread, -1e30))


def ssm_kernel(heads, x_ref, w_ref, r_ref, dt_ref, cum_ref, across_ref, s_ref, skip_ref, y_ref):
    tokens = x_ref.shape[0]
    size = x_ref.shape[1] // heads
    chunk = min(GROUP, tokens)
    for top in range(0, tokens, chunk):
        below = top + chunk
        scores = contract_last(r_ref[top:below, :], w_ref[0:below, :])
        for h in range(heads):
            span = slice(h * size, (h + 1) * size)
            inputs = x_ref[0:below, span].astype(jnp.float32)
            mixing = (scores * decay_part(cum_ref, across_ref, h, top, below)).astype(jnp.bfloat16)
            driven = (inputs * dt_ref[0:below, h : h + 1]).astype(jnp.bfloat16)
            result = jnp.dot(mixing, driven, preferred_element_type=jnp.float32)
            carried = contract_last(r_ref[top:below, :], s_ref[span, :])
            result = result + jnp.exp(cum_ref[top:below, h : h + 1]) * carried
            y_ref[top:below, span] = result + skip_ref[0:1, h : h + 1] * inputs[top:below]


def ssm_forward(inputs, writers, readers, deltas, cum, across, entering, skipping):
    heads = deltas.shape[1]
    return pl.pallas_call(
        functools.partial(ssm_kernel, heads),
        out_shape=jax.ShapeDtypeStruct(inputs.shape, jnp.float32),
        compiler_params=pltpu.CompilerParams(vmem_limit_bytes=VMEM_LIMIT),
    )(inputs, writers, readers, deltas, cum, across, entering, skipping)


def back_kernel(
    heads,
    x_ref,
    w_ref,
    r_ref,
    dt_ref,
    cum_ref,
    across_ref,
    s_ref,
    skip_ref,
    y_ref,
    dy_ref,
    l_ref,
    dx_ref,
    dw_ref,
    dr_ref,
    col_ref,
    mix_ref,
    back_ref,
):
    tokens = x_ref.shape[0]
    size = x_ref.shape[1] // heads
    chunk = min(GROUP, tokens)
    f32, b16 = jnp.float32, jnp.bfloat16
    for top in range(0, tokens, chunk):
        below = top + chunk
        scores = contract_last(r_ref[top:below, :], w_ref[0:below, :])
        for h in range(heads):
            span = slice(h * size, (h + 1) * size)
            decay = decay_part(cum_ref, across_ref, h, top, below)
            mixing = (scores * decay).astype(b16)
            driven = (x_ref[0:below, span].astype(f32) * dt_ref[0:below, h : h + 1]).astype(b16)
            grads = dy_ref[top:below, span].astype(b16)
            share = contract_last(grads, driven) * decay
            if h == 0:
                mix_ref[:, 0:below] = share
            else:
                mix_ref[:, 0:below] += share
            back = contract_first(mixing, grads)
            if top:
                back_ref[0:top, span] += back[0:top]
            back_ref[top:below, span] = back[top:below]
        mixed = mix_ref[:, 0:below].astype(b16)
        dr_ref[top:below, :] = jnp.dot(mixed, w_ref[0:below, :], preferred_element_type=f32)
        written = contract_first(mixed, r_ref[top:below, :])
        if top:
            dw_ref[0:top, :] += written[0:top]
        dw_ref[top:below, :] = written[top:below]
    for h in range(heads):
        span = slice(h * size, (h + 1) * size)
        step = dt_ref[:, h : h + 1]
        run = cum_ref[:, h : h + 1]
        skipping = skip_ref[0:1, h : h + 1]
        inputs = x_ref[:, span].astype(f32)
        grads = dy_ref[:, span]
        rounded = grads.astype(b16).astype(f32)
        driven = (inputs * step).astype(b16).astype(f32)
        left = jnp.exp(run[tokens - 1 : tokens, :] - run)
        later = left * contract_last(w_ref[...], l_ref[span, :])
        inner = back_ref[:, span]
        both = inner + later
        dx_ref[:, span] = step * both + skipping * grads
        dr_ref[...] += jnp.dot(
            (jnp.exp(run) * grads).astype(b16), s_ref[span, :], preferred_element_type=f32
        )
        dw_ref[...] += jnp.dot(
            (left * driven).astype(b16), l_ref[span, :], preferred_element_type=f32
        )
        alone = y_ref[:, span] - skipping * inputs
        col_ref[:, h : h + 1] = jnp.sum(rounded * alone - driven * both, axis=1, keepdims=True)
        col_ref[:, heads + h : heads + h + 1] = jnp.sum(inputs * both, axis=1, keepdims=True)
        at = 2 * heads + h
        col_ref[:, at : at + 1] = jnp.sum(driven * later, axis=1, keepdims=True)
        at = 3 * heads + h
        col_ref[:, at : at + 1] = jnp.sum(inputs * grads, axis=1, keepdims=True)


def ssm_backward(
    inputs, writers, readers, deltas, cum, across, entering, skipping, mixed, mixed_grad, leaving
):
    tokens, heads = deltas.shape
    chunk = min(GROUP, tokens)
    return pl.pallas_call(
        functools.partial(back_kernel, heads),
        out_shape=(
            jax.ShapeDtypeStruct(inputs.shape, jnp.float32),
            jax.ShapeDtypeStruct(writers.shape, jnp.float32),
            jax.ShapeDtypeStruct(readers.shape, jnp.float32),
            jax.ShapeDtypeStruct((tokens, 4 * heads), jnp.float32),
        ),
        scratch_shapes=[
            pltpu.VMEM((chunk, tokens), jnp.float32),
            pltpu.VMEM(inputs.shape, jnp.float32),
        ],
        compiler_params=pltpu.CompilerParams(vmem_limit_bytes=VMEM_LIMIT),
    )(
        inputs,
        writers,
        readers,
        deltas,
        cum,
        across,
        entering,
        skipping,
        mixed,
        mixed_grad,
        leaving,
    )


def swish_slope(values):
    sigma = jax.nn.sigmoid(values)
    return sigma * (1.0 + values * (1.0 - sigma))


def contract_last(former, latter):
    return lax.dot_general(
        former, latter, (((1,), (1,)), ((), ())), preferred_element_type=jnp.float32
    )


def contract_first(former, latter):
    return lax.dot_general(
        former, latter, (((0,), (0,)), ((), ())), preferred_element_type=jnp.float32
    )


def local(
    hidden,
    prescale,
    gating,
    feature,
    selective,
    timestep,
    filters,
    statefilters,
    offsets,
    stateoffsets,
    stepbias,
    decaylog,
    skipgain,
    postscale,
    projection,
    cotangent,
):
    seqcount, tokens, modelwidth = hidden.shape
    heads_here = stepbias.shape[0]
    inner_here = gating.shape[1]
    headsize = inner_here // heads_here
    statesize = selective.shape[1] // 2
    tapcount = filters.shape[0]
    rowcount = seqcount * tokens
    inner_all = inner_here * lax.axis_size("head")
    flat_in = hidden.reshape(rowcount, modelwidth).astype(jnp.float32)
    rowscale = lax.rsqrt(jnp.mean(flat_in * flat_in, axis=1, keepdims=True) + eps_norm)
    normed = (flat_in * rowscale * prescale[None, :]).astype(jnp.bfloat16)
    gate_raw = jnp.dot(normed, gating, preferred_element_type=jnp.float32)
    inner_pre = jnp.dot(normed, feature, preferred_element_type=jnp.float32).astype(jnp.bfloat16)
    state_pre = jnp.dot(normed, selective, preferred_element_type=jnp.float32).astype(jnp.bfloat16)
    step_raw = jnp.dot(normed, timestep, preferred_element_type=jnp.float32)
    channels = jnp.concatenate([inner_pre, state_pre], axis=1).reshape(
        seqcount, tokens, inner_here + 2 * statesize
    )
    edge_in = passed_along(channels[:, tokens - tapcount + 1 :, :], "seq", 1)
    padded = jnp.concatenate([edge_in, channels], axis=1).astype(jnp.float32)
    kernel = jnp.concatenate([filters, statefilters], axis=1)
    shifts = jnp.concatenate([offsets, stateoffsets], axis=0)
    filtered = shifts[None, None, :] + kernel[0][None, None, :] * padded[:, 0:tokens]
    for tapindex in range(1, tapcount):
        filtered = (
            filtered + kernel[tapindex][None, None, :] * padded[:, tapindex : tapindex + tokens]
        )
    activity = jax.nn.silu(filtered).astype(jnp.bfloat16)[0]
    inner_x = activity[:, :inner_here]
    writers = activity[:, inner_here : inner_here + statesize]
    readers = activity[:, inner_here + statesize :]
    step_sum = step_raw + stepbias[None, :]
    deltas = jax.nn.softplus(step_sum)
    rates = -jnp.exp(decaylog)
    causal = (
        lax.broadcasted_iota(jnp.int32, (tokens, tokens), 0)
        >= lax.broadcasted_iota(jnp.int32, (tokens, tokens), 1)
    ).astype(jnp.float32)
    running = jnp.dot(causal, deltas * rates[None, :], precision=exact)
    across = running.T
    finale = running[-1]
    overall = jnp.exp(finale)
    skipping = skipgain[None, :]
    local_end = weighted_states(inner_x, jnp.exp(finale[None, :] - running) * deltas, writers)
    state_shape = (heads_here, headsize, statesize)
    entering = relayed(local_end.reshape(state_shape), overall, "seq", False, 0)
    flat_entering = entering.reshape(inner_here, statesize)
    mixed = ssm_forward(
        inner_x, writers, readers, deltas, running, across, flat_entering, skipping
    )
    upstream = lax.all_gather(cotangent, "head", axis=2, tiled=True).reshape(rowcount, modelwidth)
    normed_out_grad = jnp.dot(upstream, projection, preferred_element_type=jnp.float32)
    scaled_grad = normed_out_grad * postscale[None, :]
    gate_act = jax.nn.silu(gate_raw)
    gated = mixed * gate_act
    sums = jnp.concatenate(
        [jnp.sum(gated * gated, axis=1), jnp.sum(scaled_grad * gated, axis=1)]
    ).reshape(-1, 128)
    sums = jnp.sum(gathered(sums, "head", 1), axis=0).reshape(2, rowcount)
    row_terms = sums[1]
    gated_scale = lax.rsqrt(sums[0][:, None] / inner_all + eps_norm)
    normed_out = (gated * gated_scale * postscale[None, :]).astype(jnp.bfloat16)
    partial_out = contract_last(normed_out, projection)
    out_share = lax.psum_scatter(
        partial_out.astype(jnp.bfloat16), "head", scatter_dimension=1, tiled=True
    ).astype(jnp.float32)
    quarter = out_share.shape[1]
    residual = lax.dynamic_slice_in_dim(flat_in, lax.axis_index("head") * quarter, quarter, 1)
    output = (residual + out_share).astype(jnp.bfloat16).reshape(seqcount, tokens, quarter)
    projection_grad = contract_first(upstream, normed_out)
    postscale_grad = jnp.sum(normed_out_grad * gated * gated_scale, axis=0)
    gated_grad = gated_scale * scaled_grad - gated * gated_scale**3 * row_terms[:, None] / inner_all
    mixed_grad = gated_grad * gate_act
    gate_grad = (gated_grad * mixed * swish_slope(gate_raw)).astype(jnp.bfloat16)
    carry_entering = weighted_states(mixed_grad, jnp.exp(running), readers)
    leaving = relayed(carry_entering.reshape(state_shape), overall, "seq", True, 2)
    local_inner, writers_grad, readers_grad, terms = ssm_backward(
        inner_x,
        writers,
        readers,
        deltas,
        running,
        across,
        flat_entering,
        skipping,
        mixed,
        mixed_grad,
        leaving.reshape(inner_here, statesize),
    )
    at_end = jnp.sum(terms[:, 2 * heads_here : 3 * heads_here], axis=0) + overall * jnp.sum(
        entering.astype(jnp.float32) * leaving.astype(jnp.float32), axis=(1, 2)
    )
    decays_grad = at_end[None, :] + lax.dot_general(
        causal, terms[:, :heads_here], (((0,), (0,)), ((), ())), precision=exact
    )
    deltas_grad = terms[:, heads_here : 2 * heads_here] + rates[None, :] * decays_grad
    skipgain_grad = jnp.sum(terms[:, 3 * heads_here :], axis=0)
    decaylog_grad = jnp.sum(deltas * decays_grad, axis=0) * rates
    step_full = deltas_grad * jax.nn.sigmoid(step_sum)
    stepbias_grad = jnp.sum(step_full, axis=0)
    step_grad = step_full.astype(jnp.bfloat16)
    state_act_grad = jnp.concatenate([writers_grad, readers_grad], axis=1)
    state_act_grad = summed(state_act_grad.astype(jnp.bfloat16), "head", 3).astype(jnp.float32)
    local_inner = local_inner[None]
    state_act_grad = state_act_grad[None]
    act_grad = jnp.concatenate([local_inner, state_act_grad], axis=2)
    filtered_grad = act_grad * swish_slope(filtered)
    kernel_grad = jnp.stack(
        [
            jnp.sum(padded[:, tapindex : tapindex + tokens] * filtered_grad, axis=(0, 1))
            for tapindex in range(tapcount)
        ]
    )
    shifts_grad = jnp.sum(filtered_grad, axis=(0, 1))
    padded_grad = jnp.pad(
        kernel[0][None, None, :] * filtered_grad, ((0, 0), (0, tapcount - 1), (0, 0))
    )
    for tapindex in range(1, tapcount):
        padded_grad = padded_grad + jnp.pad(
            kernel[tapindex][None, None, :] * filtered_grad,
            ((0, 0), (tapindex, tapcount - 1 - tapindex), (0, 0)),
        )
    edge_back = passed_along(padded_grad[:, : tapcount - 1], "seq", -1)
    channel_grad = padded_grad[:, tapcount - 1 :] + jnp.pad(
        edge_back, ((0, 0), (tokens - tapcount + 1, 0), (0, 0))
    )
    inner_pre_grad = (
        channel_grad[:, :, :inner_here].reshape(rowcount, inner_here).astype(jnp.bfloat16)
    )
    state_pre_grad = channel_grad[:, :, inner_here:].reshape(rowcount, 2 * statesize)
    partial_in = (
        contract_last(gate_grad, gating)
        + contract_last(inner_pre_grad, feature)
        + contract_last(step_grad, timestep)
    )
    state_term = lax.dot_general(
        state_pre_grad, selective.astype(jnp.float32), (((1,), (1,)), ((), ())), precision=exact
    )
    mine = 2 * statesize // lax.axis_size("head")
    state_share = lax.dynamic_slice_in_dim(
        state_pre_grad, lax.axis_index("head") * mine, mine, 1
    )
    selective_grad = lax.dot_general(
        normed.astype(jnp.float32), state_share, (((0,), (0,)), ((), ())), precision=exact
    )
    statefilters_grad = kernel_grad[:, inner_here:]
    stateoffsets_grad = shifts_grad[inner_here:]
    gating_grad = contract_first(normed, gate_grad)
    feature_grad = contract_first(normed, inner_pre_grad)
    timestep_grad = contract_first(normed, step_grad)
    narrow = jnp.concatenate([selective_grad, timestep_grad], axis=1).astype(jnp.bfloat16)
    narrow = jnp.pad(narrow, ((0, 0), (0, -narrow.shape[1] % 128)))
    normed_grad, (projection_grad, gating_grad, feature_grad, narrow) = finished_sums(
        partial_in.astype(jnp.bfloat16),
        (
            projection_grad.astype(jnp.bfloat16),
            gating_grad.astype(jnp.bfloat16),
            feature_grad.astype(jnp.bfloat16),
            narrow,
        ),
        4,
    )
    normed_grad = normed_grad.astype(jnp.float32) + state_term
    prescale_grad = jnp.sum(normed_grad * flat_in * rowscale, axis=0)
    scaled_in = normed_grad * prescale[None, :]
    row_in = jnp.sum(scaled_in * flat_in, axis=1, keepdims=True)
    hidden_grad = (
        upstream.astype(jnp.float32)
        + rowscale * scaled_in
        - flat_in * rowscale**3 * row_in / modelwidth
    )
    hidden_grad = hidden_grad.reshape(seqcount, tokens, modelwidth)
    timestep_grad = narrow[:, mine : mine + heads_here]
    around = gathered(narrow.astype(jnp.bfloat16), "head", 5)[:, :, :mine]
    selective_grad = (
        around.transpose(1, 0, 2).reshape(narrow.shape[0], 2 * statesize).astype(jnp.float32)
    )
    small = (
        kernel_grad[:, :inner_here],
        statefilters_grad,
        shifts_grad[:inner_here],
        stateoffsets_grad,
        postscale_grad,
        prescale_grad,
        stepbias_grad,
        decaylog_grad,
        skipgain_grad,
    )
    packed = jnp.concatenate([part.reshape(-1) for part in small])
    packed = jnp.pad(packed, (0, -packed.shape[0] % 1024)).reshape(-1, 128)
    packed = jnp.sum(gathered(packed, "seq", 6), axis=0).reshape(-1)
    at, finished = 0, []
    for part in small:
        finished.append(packed[at : at + part.size].reshape(part.shape))
        at += part.size
    (
        filters_grad,
        statefilters_grad,
        offsets_grad,
        stateoffsets_grad,
        postscale_grad,
        prescale_grad,
        stepbias_grad,
        decaylog_grad,
        skipgain_grad,
    ) = finished
    owned = modelwidth // lax.axis_size("seq")
    prescale_grad = lax.dynamic_slice_in_dim(
        prescale_grad, lax.axis_index("seq") * owned, owned, 0
    )
    return (
        output,
        hidden_grad,
        prescale_grad,
        gating_grad,
        feature_grad,
        selective_grad,
        timestep_grad,
        filters_grad,
        statefilters_grad,
        offsets_grad,
        stateoffsets_grad,
        stepbias_grad,
        decaylog_grad,
        skipgain_grad,
        postscale_grad,
        projection_grad,
    )


def solution(mesh):
    placed = (
        P(None, "seq", None),
        P(),
        P(None, "head"),
        P(None, "head"),
        P(),
        P(None, "head"),
        P(None, "head"),
        P(),
        P("head"),
        P(),
        P("head"),
        P("head"),
        P("head"),
        P("head"),
        P(None, "head"),
        P(None, "seq", "head"),
    )
    return jax.shard_map(
        local,
        mesh=mesh,
        in_specs=placed,
        out_specs=(
            P(None, "seq", "head"),
            P(None, "seq", None),
            P("seq"),
            P("seq", "head"),
            P("seq", "head"),
            P("seq", None),
            P("seq", "head"),
            P(None, "head"),
            P(),
            P("head"),
            P(),
            P("head"),
            P("head"),
            P("head"),
            P("head"),
            P("seq", "head"),
        ),
        check_vma=False,
    )
```

```python
import functools

import jax
import jax.numpy as jnp
from jax import lax
from jax.experimental import pallas as pl
from jax.experimental.pallas import tpu as pltpu
from jax.sharding import PartitionSpec as P

GROUP = 256
VMEM_LIMIT = 48 * 2**20


eps_norm = 1e-05
exact = lax.Precision.HIGHEST


def passed_along(shard, axis, by):
    count = lax.axis_size(axis)
    pairs = [(i, i + by) for i in range(count) if 0 <= i + by < count]
    return lax.ppermute(shard, axis, pairs)


def greet(axis, n):
    me = lax.axis_index(axis)
    barrier = pltpu.get_barrier_semaphore()
    for k in range(1, n):
        pl.semaphore_signal(
            barrier,
            inc=1,
            device_id={axis: lax.rem(me + k, n)},
            device_id_type=pl.DeviceIdType.MESH,
        )
    pl.semaphore_wait(barrier, n - 1)
    return me


def push(source, target, sends, arrivals, k, axis, n):
    copy = pltpu.make_async_remote_copy(
        src_ref=source,
        dst_ref=target,
        send_sem=sends.at[k],
        recv_sem=arrivals.at[k],
        device_id={axis: lax.rem(lax.axis_index(axis) + k, n)},
        device_id_type=pl.DeviceIdType.MESH,
    )
    copy.start()
    return copy


def gather_kernel(axis, n, x_ref, o_ref, sends, arrivals):
    me = greet(axis, n)
    copies = [push(x_ref, o_ref.at[me], sends, arrivals, k, axis, n) for k in range(1, n)]
    o_ref[me] = x_ref[...]
    for copy in copies:
        copy.wait()


def gathered(x, axis, ident):
    n = lax.axis_size(axis)
    if n > 8:
        return lax.all_gather(x, axis)
    return pl.pallas_call(
        functools.partial(gather_kernel, axis, n),
        out_shape=jax.ShapeDtypeStruct((n, *x.shape), x.dtype),
        in_specs=[pl.BlockSpec(memory_space=pltpu.VMEM)],
        out_specs=pl.BlockSpec(memory_space=pltpu.VMEM),
        scratch_shapes=[pltpu.SemaphoreType.DMA((n,)), pltpu.SemaphoreType.DMA((n,))],
        compiler_params=pltpu.CompilerParams(
            collective_id=ident, has_side_effects=True, vmem_limit_bytes=VMEM_LIMIT
        ),
    )(x)


def allsum_kernel(axis, n, x_ref, o_ref, landed, send1, recv1, send2, recv2):
    me = greet(axis, n)
    firsts = [
        push(x_ref.at[lax.rem(me + k, n)], landed.at[k], send1, recv1, k, axis, n)
        for k in range(1, n)
    ]
    for copy in firsts:
        copy.wait()
    total = x_ref[me].astype(jnp.float32)
    for k in range(1, n):
        total = total + landed[k].astype(jnp.float32)
    o_ref[me] = total.astype(o_ref.dtype)
    seconds = [push(o_ref.at[me], o_ref.at[me], send2, recv2, k, axis, n) for k in range(1, n)]
    for copy in seconds:
        copy.wait()


def summed(x, axis, ident):
    n = lax.axis_size(axis)
    rows, columns = x.shape
    if n > 8 or rows % (16 * n):
        return lax.psum(x, axis)
    piece = (n, rows // n, columns)
    return pl.pallas_call(
        functools.partial(allsum_kernel, axis, n),
        out_shape=jax.ShapeDtypeStruct(piece, x.dtype),
        in_specs=[pl.BlockSpec(memory_space=pltpu.VMEM)],
        out_specs=pl.BlockSpec(memory_space=pltpu.VMEM),
        scratch_shapes=[pltpu.VMEM(piece, x.dtype)] + [pltpu.SemaphoreType.DMA((n,))] * 4,
        compiler_params=pltpu.CompilerParams(
            collective_id=ident, has_side_effects=True, vmem_limit_bytes=VMEM_LIMIT
        ),
    )(x.reshape(piece)).reshape(rows, columns)


def remote(source, target, send, arrival, axis, index):
    copy = pltpu.make_async_remote_copy(
        src_ref=source,
        dst_ref=target,
        send_sem=send,
        recv_sem=arrival,
        device_id={axis: index},
        device_id_type=pl.DeviceIdType.MESH,
    )
    copy.start()
    return copy


def finish_kernel(heads, n, count, work, *refs):
    t_ref, x_refs = refs[0], refs[1 : 1 + count]
    refs = refs[1 + count :]
    sum_ref, o_refs = refs[0], refs[1 : 1 + count]
    refs = refs[1 + count :]
    landed, near, parts, far = (
        refs[0],
        refs[1 : 1 + count],
        refs[1 + count : 1 + 2 * count],
        refs[1 + 2 * count : 1 + 3 * count],
    )
    hs1, hr1, hs2, hr2, s1, r1, s2, r2 = refs[1 + 3 * count :]
    across, along = lax.axis_index("head"), lax.axis_index("seq")
    half = n // 2
    row, side = along // 2, along % 2
    partner = 2 * row + 1 - side
    barrier = pltpu.get_barrier_semaphore()
    greeted = [("head", lax.rem(across + k, heads)) for k in range(1, heads)]
    greeted.append(("seq", partner))
    greeted += [("seq", 2 * lax.rem(row + k, half) + side) for k in range(1, half)]
    for axis, index in greeted:
        pl.semaphore_signal(
            barrier, inc=1, device_id={axis: index}, device_id_type=pl.DeviceIdType.MESH
        )
    pl.semaphore_wait(barrier, len(greeted))
    first = []
    for c in range(count):
        first.append(
            [
                remote(
                    x_refs[c].at[2 * j + 1 - side],
                    near[c].at[j],
                    s1.at[c, j],
                    r1.at[c, j],
                    "seq",
                    partner,
                )
                for j in range(half)
            ]
        )
    if work is not None:
        work()
    turn = []
    for k in range(1, heads):
        peer = lax.rem(across + k, heads)
        turn.append(remote(t_ref.at[peer], landed.at[k], hs1.at[k], hr1.at[k], "head", peer))

    def second(c):
        for copy in first[c]:
            copy.wait()
        for j in range(half):
            total = x_refs[c][2 * j + side].astype(jnp.float32) + near[c][j].astype(jnp.float32)
            parts[c][j] = total.astype(jnp.bfloat16)
        copies = []
        for k in range(1, half):
            peer = lax.rem(row + k, half)
            copies.append(
                remote(
                    parts[c].at[peer],
                    far[c].at[k],
                    s2.at[c, k],
                    r2.at[c, k],
                    "seq",
                    2 * peer + side,
                )
            )
        return copies

    later = [second(0)]
    for copy in turn:
        copy.wait()
    total = t_ref[across].astype(jnp.float32)
    for k in range(1, heads):
        total = total + landed[k].astype(jnp.float32)
    sum_ref[across] = total.astype(jnp.bfloat16)
    back = []
    for k in range(1, heads):
        peer = lax.rem(across + k, heads)
        back.append(
            remote(sum_ref.at[across], sum_ref.at[across], hs2.at[k], hr2.at[k], "head", peer)
        )
    for c in range(1, count):
        later.append(second(c))
    for c in range(count):
        for copy in later[c]:
            copy.wait()
        total = parts[c][row].astype(jnp.float32)
        for k in range(1, half):
            total = total + far[c][k].astype(jnp.float32)
        o_refs[c][...] = total
    for copy in back:
        copy.wait()


def finished_sums(terms, grads, ident):
    heads, n = lax.axis_size("head"), lax.axis_size("seq")
    rows, columns = terms.shape
    if n > 8 or n % 2 or rows % (16 * heads) or grads[0].shape[0] % (16 * n):
        shares = [
            lax.psum_scatter(part, "seq", scatter_dimension=0, tiled=True).astype(jnp.float32)
            for part in grads
        ]
        return summed(terms, "head", ident), shares
    count, half = len(grads), n // 2
    piece = (heads, rows // heads, columns)
    blocks = [(part.shape[0] // n, part.shape[1]) for part in grads]
    vmem = pl.BlockSpec(memory_space=pltpu.VMEM)
    landing = [pltpu.VMEM((half, *block), jnp.bfloat16) for block in blocks]
    total, *shares = pl.pallas_call(
        functools.partial(finish_kernel, heads, n, count, None),
        out_shape=(
            jax.ShapeDtypeStruct(piece, jnp.bfloat16),
            *(jax.ShapeDtypeStruct(block, jnp.float32) for block in blocks),
        ),
        in_specs=[vmem] * (1 + count),
        out_specs=(vmem,) * (1 + count),
        scratch_shapes=[pltpu.VMEM(piece, jnp.bfloat16)]
        + landing * 3
        + [pltpu.SemaphoreType.DMA((heads,))] * 4
        + [pltpu.SemaphoreType.DMA((count, half))] * 4,
        compiler_params=pltpu.CompilerParams(
            collective_id=ident, has_side_effects=True, vmem_limit_bytes=VMEM_LIMIT
        ),
    )(
        terms.reshape(piece),
        *(part.reshape(n, *block) for part, block in zip(grads, blocks)),
    )
    return total.reshape(rows, columns), shares


def relay_kernel(axis, n, backwards, s_ref, d_ref, o_ref, s_in, d_in, out, sends, recvs):
    me = greet(axis, n)
    firsts = []
    for k in range(1, n):
        peer = lax.rem(me + k, n)
        firsts.append(push(d_ref.at[peer], d_in.at[me], sends.at[0], recvs.at[0], k, axis, n))
        firsts.append(push(s_ref.at[peer], s_in.at[me], sends.at[1], recvs.at[1], k, axis, n))
    d_in[me] = d_ref[me]
    s_in[me] = s_ref[me]
    for copy in firsts:
        copy.wait()
    total = jnp.zeros(s_ref.shape[1:], jnp.float32)
    for p in range(n - 1, -1, -1) if backwards else range(n):
        out[p] = total.astype(out.dtype)
        total = d_in[p][0:1, :] * total + s_in[p].astype(jnp.float32)
    o_ref[me] = out[me]
    seconds = [
        push(out.at[lax.rem(me + k, n)], o_ref.at[me], sends.at[2], recvs.at[2], k, axis, n)
        for k in range(1, n)
    ]
    for copy in seconds:
        copy.wait()


def relayed(states, decays, axis, backwards, ident):
    n = lax.axis_size(axis)
    heads, rows, columns = states.shape
    if heads != n:
        place = lax.axis_index(axis)
        allstates = lax.all_gather(states.astype(jnp.bfloat16), axis)
        alldecays = lax.all_gather(decays, axis)

        def hop(k, total):
            source = n - 1 - k if backwards else k
            reached = source > place if backwards else source < place
            new = alldecays[source][:, None, None] * total + allstates[source].astype(jnp.float32)
            return jnp.where(reached, new, total)

        return lax.fori_loop(0, n, hop, jnp.zeros(states.shape, jnp.float32)).astype(jnp.bfloat16)
    return pl.pallas_call(
        functools.partial(relay_kernel, axis, n, backwards),
        out_shape=jax.ShapeDtypeStruct(states.shape, jnp.bfloat16),
        in_specs=[pl.BlockSpec(memory_space=pltpu.VMEM)] * 2,
        out_specs=pl.BlockSpec(memory_space=pltpu.VMEM),
        scratch_shapes=[
            pltpu.VMEM(states.shape, jnp.bfloat16),
            pltpu.VMEM((n, 8, columns), jnp.float32),
            pltpu.VMEM(states.shape, jnp.bfloat16),
            pltpu.SemaphoreType.DMA((3, n)),
            pltpu.SemaphoreType.DMA((3, n)),
        ],
        compiler_params=pltpu.CompilerParams(
            collective_id=ident, has_side_effects=True, vmem_limit_bytes=VMEM_LIMIT
        ),
    )(
        states.astype(jnp.bfloat16),
        jnp.broadcast_to(decays[:, None, None], (n, 8, columns)),
    )


def states_kernel(heads, v_ref, w_ref, b_ref, o_ref):
    size = v_ref.shape[1] // heads
    columns = b_ref[...]
    for h in range(heads):
        span = slice(h * size, (h + 1) * size)
        weighted = v_ref[:, span].astype(jnp.float32) * w_ref[:, h : h + 1]
        o_ref[span, :] = contract_first(weighted.astype(jnp.bfloat16), columns).astype(o_ref.dtype)


def weighted_states(values, weights, columns):
    heads = weights.shape[1]
    return pl.pallas_call(
        functools.partial(states_kernel, heads),
        out_shape=jax.ShapeDtypeStruct((values.shape[1], columns.shape[1]), jnp.bfloat16),
        compiler_params=pltpu.CompilerParams(vmem_limit_bytes=VMEM_LIMIT),
    )(values, weights, columns)


def decay_part(cum_ref, across_ref, h, top, below):
    rows = lax.broadcasted_iota(jnp.int32, (below - top, below), 0) + top
    columns = lax.broadcasted_iota(jnp.int32, (below - top, below), 1)
    spread = cum_ref[top:below, h : h + 1] - across_ref[h : h + 1, 0:below]
    return jnp.exp(jnp.where(rows >= columns, spread, -1e30))


def ssm_kernel(heads, x_ref, w_ref, r_ref, dt_ref, cum_ref, across_ref, s_ref, skip_ref, y_ref):
    tokens = x_ref.shape[0]
    size = x_ref.shape[1] // heads
    chunk = min(GROUP, tokens)
    for top in range(0, tokens, chunk):
        below = top + chunk
        scores = contract_last(r_ref[top:below, :], w_ref[0:below, :])
        for h in range(heads):
            span = slice(h * size, (h + 1) * size)
            inputs = x_ref[0:below, span].astype(jnp.float32)
            mixing = (scores * decay_part(cum_ref, across_ref, h, top, below)).astype(jnp.bfloat16)
            driven = (inputs * dt_ref[0:below, h : h + 1]).astype(jnp.bfloat16)
            result = jnp.dot(mixing, driven, preferred_element_type=jnp.float32)
            carried = contract_last(r_ref[top:below, :], s_ref[span, :])
            result = result + jnp.exp(cum_ref[top:below, h : h + 1]) * carried
            y_ref[top:below, span] = result + skip_ref[0:1, h : h + 1] * inputs[top:below]


def ssm_forward(inputs, writers, readers, deltas, cum, across, entering, skipping):
    heads = deltas.shape[1]
    return pl.pallas_call(
        functools.partial(ssm_kernel, heads),
        out_shape=jax.ShapeDtypeStruct(inputs.shape, jnp.float32),
        compiler_params=pltpu.CompilerParams(vmem_limit_bytes=VMEM_LIMIT),
    )(inputs, writers, readers, deltas, cum, across, entering, skipping)


def back_kernel(
    heads,
    x_ref,
    w_ref,
    r_ref,
    dt_ref,
    cum_ref,
    across_ref,
    s_ref,
    skip_ref,
    y_ref,
    dy_ref,
    l_ref,
    dx_ref,
    dw_ref,
    dr_ref,
    col_ref,
    mix_ref,
    back_ref,
):
    tokens = x_ref.shape[0]
    size = x_ref.shape[1] // heads
    chunk = min(GROUP, tokens)
    f32, b16 = jnp.float32, jnp.bfloat16
    for top in range(0, tokens, chunk):
        below = top + chunk
        scores = contract_last(r_ref[top:below, :], w_ref[0:below, :])
        for h in range(heads):
            span = slice(h * size, (h + 1) * size)
            decay = decay_part(cum_ref, across_ref, h, top, below)
            mixing = (scores * decay).astype(b16)
            driven = (x_ref[0:below, span].astype(f32) * dt_ref[0:below, h : h + 1]).astype(b16)
            grads = dy_ref[top:below, span].astype(b16)
            share = contract_last(grads, driven) * decay
            if h == 0:
                mix_ref[:, 0:below] = share
            else:
                mix_ref[:, 0:below] += share
            back = contract_first(mixing, grads)
            if top:
                back_ref[0:top, span] += back[0:top]
            back_ref[top:below, span] = back[top:below]
        mixed = mix_ref[:, 0:below].astype(b16)
        dr_ref[top:below, :] = jnp.dot(mixed, w_ref[0:below, :], preferred_element_type=f32)
        written = contract_first(mixed, r_ref[top:below, :])
        if top:
            dw_ref[0:top, :] += written[0:top]
        dw_ref[top:below, :] = written[top:below]
    for h in range(heads):
        span = slice(h * size, (h + 1) * size)
        step = dt_ref[:, h : h + 1]
        run = cum_ref[:, h : h + 1]
        skipping = skip_ref[0:1, h : h + 1]
        inputs = x_ref[:, span].astype(f32)
        grads = dy_ref[:, span]
        rounded = grads.astype(b16).astype(f32)
        driven = (inputs * step).astype(b16).astype(f32)
        left = jnp.exp(run[tokens - 1 : tokens, :] - run)
        later = left * contract_last(w_ref[...], l_ref[span, :])
        inner = back_ref[:, span]
        both = inner + later
        dx_ref[:, span] = step * both + skipping * grads
        dr_ref[...] += jnp.dot(
            (jnp.exp(run) * grads).astype(b16), s_ref[span, :], preferred_element_type=f32
        )
        dw_ref[...] += jnp.dot(
            (left * driven).astype(b16), l_ref[span, :], preferred_element_type=f32
        )
        alone = y_ref[:, span] - skipping * inputs
        col_ref[:, h : h + 1] = jnp.sum(rounded * alone - driven * both, axis=1, keepdims=True)
        col_ref[:, heads + h : heads + h + 1] = jnp.sum(inputs * both, axis=1, keepdims=True)
        at = 2 * heads + h
        col_ref[:, at : at + 1] = jnp.sum(driven * later, axis=1, keepdims=True)
        at = 3 * heads + h
        col_ref[:, at : at + 1] = jnp.sum(inputs * grads, axis=1, keepdims=True)


def ssm_backward(
    inputs, writers, readers, deltas, cum, across, entering, skipping, mixed, mixed_grad, leaving
):
    tokens, heads = deltas.shape
    chunk = min(GROUP, tokens)
    return pl.pallas_call(
        functools.partial(back_kernel, heads),
        out_shape=(
            jax.ShapeDtypeStruct(inputs.shape, jnp.float32),
            jax.ShapeDtypeStruct(writers.shape, jnp.float32),
            jax.ShapeDtypeStruct(readers.shape, jnp.float32),
            jax.ShapeDtypeStruct((tokens, 4 * heads), jnp.float32),
        ),
        scratch_shapes=[
            pltpu.VMEM((chunk, tokens), jnp.float32),
            pltpu.VMEM(inputs.shape, jnp.float32),
        ],
        compiler_params=pltpu.CompilerParams(vmem_limit_bytes=VMEM_LIMIT),
    )(
        inputs,
        writers,
        readers,
        deltas,
        cum,
        across,
        entering,
        skipping,
        mixed,
        mixed_grad,
        leaving,
    )


def swish_slope(values):
    sigma = jax.nn.sigmoid(values)
    return sigma * (1.0 + values * (1.0 - sigma))


def contract_last(former, latter):
    return lax.dot_general(
        former, latter, (((1,), (1,)), ((), ())), preferred_element_type=jnp.float32
    )


def contract_first(former, latter):
    return lax.dot_general(
        former, latter, (((0,), (0,)), ((), ())), preferred_element_type=jnp.float32
    )


def back_send_kernel(own, heads, n, count, *refs):
    ins, grads, refs = refs[:11], refs[11 : 11 + count], refs[11 + count :]
    outs, sums, refs = refs[:4], refs[4 : 5 + count], refs[5 + count :]
    landing, (mix_ref, back_ref, t_ref) = refs[:-3], refs[-3:]

    def work():
        back_kernel(own, *ins, *outs, mix_ref, back_ref)
        rows, states = t_ref.shape[1], outs[1].shape[1]
        for p in range(heads):
            span = slice(p * rows, (p + 1) * rows)
            t_ref[p, :, 0:states] = outs[1][span, :].astype(jnp.bfloat16)
            t_ref[p, :, states:] = outs[2][span, :].astype(jnp.bfloat16)

    finish_kernel(heads, n, count, work, t_ref, *grads, *sums, *landing)


def backward_and_sums(operands, grads, ident):
    heads, n = lax.axis_size("head"), lax.axis_size("seq")
    inputs, writers, deltas = operands[0], operands[1], operands[3]
    tokens, own = deltas.shape
    columns = 2 * writers.shape[1]
    if n > 8 or n % 2 or tokens % (16 * heads) or grads[0].shape[0] % (16 * n):
        shares = [
            lax.psum_scatter(part, "seq", scatter_dimension=0, tiled=True).astype(jnp.float32)
            for part in grads
        ]
        local_inner, writers_grad, readers_grad, terms = ssm_backward(*operands)
        both = jnp.concatenate([writers_grad, readers_grad], axis=1).astype(jnp.bfloat16)
        return local_inner, summed(both, "head", ident), terms, shares
    count, half = len(grads), n // 2
    piece = (heads, tokens // heads, columns)
    blocks = [(part.shape[0] // n, part.shape[1]) for part in grads]
    vmem = pl.BlockSpec(memory_space=pltpu.VMEM)
    landing = [pltpu.VMEM((half, *block), jnp.bfloat16) for block in blocks]
    local_inner, _, _, terms, total, *shares = pl.pallas_call(
        functools.partial(back_send_kernel, own, heads, n, count),
        out_shape=(
            jax.ShapeDtypeStruct(inputs.shape, jnp.float32),
            jax.ShapeDtypeStruct(writers.shape, jnp.float32),
            jax.ShapeDtypeStruct(writers.shape, jnp.float32),
            jax.ShapeDtypeStruct((tokens, 4 * own), jnp.float32),
            jax.ShapeDtypeStruct(piece, jnp.bfloat16),
            *(jax.ShapeDtypeStruct(block, jnp.float32) for block in blocks),
        ),
        in_specs=[vmem] * (len(operands) + count),
        out_specs=(vmem,) * (5 + count),
        scratch_shapes=[pltpu.VMEM(piece, jnp.bfloat16)]
        + landing * 3
        + [pltpu.SemaphoreType.DMA((heads,))] * 4
        + [pltpu.SemaphoreType.DMA((count, half))] * 4
        + [
            pltpu.VMEM((min(GROUP, tokens), tokens), jnp.float32),
            pltpu.VMEM(inputs.shape, jnp.float32),
            pltpu.VMEM(piece, jnp.bfloat16),
        ],
        compiler_params=pltpu.CompilerParams(
            collective_id=ident, has_side_effects=True, vmem_limit_bytes=VMEM_LIMIT
        ),
    )(*operands, *(part.reshape(n, *block) for part, block in zip(grads, blocks)))
    return local_inner, total.reshape(tokens, columns), terms, shares


def local(
    hidden,
    prescale,
    gating,
    feature,
    selective,
    timestep,
    filters,
    statefilters,
    offsets,
    stateoffsets,
    stepbias,
    decaylog,
    skipgain,
    postscale,
    projection,
    cotangent,
):
    seqcount, tokens, modelwidth = hidden.shape
    heads_here = stepbias.shape[0]
    inner_here = gating.shape[1]
    headsize = inner_here // heads_here
    statesize = selective.shape[1] // 2
    tapcount = filters.shape[0]
    rowcount = seqcount * tokens
    inner_all = inner_here * lax.axis_size("head")
    flat_in = hidden.reshape(rowcount, modelwidth).astype(jnp.float32)
    rowscale = lax.rsqrt(jnp.mean(flat_in * flat_in, axis=1, keepdims=True) + eps_norm)
    normed = (flat_in * rowscale * prescale[None, :]).astype(jnp.bfloat16)
    gate_raw = jnp.dot(normed, gating, preferred_element_type=jnp.float32)
    inner_pre = jnp.dot(normed, feature, preferred_element_type=jnp.float32).astype(jnp.bfloat16)
    state_pre = jnp.dot(normed, selective, preferred_element_type=jnp.float32).astype(jnp.bfloat16)
    step_raw = jnp.dot(normed, timestep, preferred_element_type=jnp.float32)
    channels = jnp.concatenate([inner_pre, state_pre], axis=1).reshape(
        seqcount, tokens, inner_here + 2 * statesize
    )
    edge_in = passed_along(channels[:, tokens - tapcount + 1 :, :], "seq", 1)
    padded = jnp.concatenate([edge_in, channels], axis=1).astype(jnp.float32)
    kernel = jnp.concatenate([filters, statefilters], axis=1)
    shifts = jnp.concatenate([offsets, stateoffsets], axis=0)
    filtered = shifts[None, None, :] + kernel[0][None, None, :] * padded[:, 0:tokens]
    for tapindex in range(1, tapcount):
        filtered = (
            filtered + kernel[tapindex][None, None, :] * padded[:, tapindex : tapindex + tokens]
        )
    activity = jax.nn.silu(filtered).astype(jnp.bfloat16)[0]
    inner_x = activity[:, :inner_here]
    writers = activity[:, inner_here : inner_here + statesize]
    readers = activity[:, inner_here + statesize :]
    step_sum = step_raw + stepbias[None, :]
    deltas = jax.nn.softplus(step_sum)
    rates = -jnp.exp(decaylog)
    causal = (
        lax.broadcasted_iota(jnp.int32, (tokens, tokens), 0)
        >= lax.broadcasted_iota(jnp.int32, (tokens, tokens), 1)
    ).astype(jnp.float32)
    running = jnp.dot(causal, deltas * rates[None, :], precision=exact)
    across = running.T
    finale = running[-1]
    overall = jnp.exp(finale)
    skipping = skipgain[None, :]
    local_end = weighted_states(inner_x, jnp.exp(finale[None, :] - running) * deltas, writers)
    state_shape = (heads_here, headsize, statesize)
    entering = relayed(local_end.reshape(state_shape), overall, "seq", False, 0)
    flat_entering = entering.reshape(inner_here, statesize)
    mixed = ssm_forward(
        inner_x, writers, readers, deltas, running, across, flat_entering, skipping
    )
    upstream = lax.all_gather(cotangent, "head", axis=2, tiled=True).reshape(rowcount, modelwidth)
    normed_out_grad = jnp.dot(upstream, projection, preferred_element_type=jnp.float32)
    scaled_grad = normed_out_grad * postscale[None, :]
    gate_act = jax.nn.silu(gate_raw)
    gated = mixed * gate_act
    sums = jnp.concatenate(
        [jnp.sum(gated * gated, axis=1), jnp.sum(scaled_grad * gated, axis=1)]
    ).reshape(-1, 128)
    sums = jnp.sum(gathered(sums, "head", 1), axis=0).reshape(2, rowcount)
    row_terms = sums[1]
    gated_scale = lax.rsqrt(sums[0][:, None] / inner_all + eps_norm)
    normed_out = (gated * gated_scale * postscale[None, :]).astype(jnp.bfloat16)
    partial_out = contract_last(normed_out, projection)
    out_share = lax.psum_scatter(
        partial_out.astype(jnp.bfloat16), "head", scatter_dimension=1, tiled=True
    ).astype(jnp.float32)
    quarter = out_share.shape[1]
    residual = lax.dynamic_slice_in_dim(flat_in, lax.axis_index("head") * quarter, quarter, 1)
    output = (residual + out_share).astype(jnp.bfloat16).reshape(seqcount, tokens, quarter)
    projection_grad = contract_first(upstream, normed_out)
    postscale_grad = jnp.sum(normed_out_grad * gated * gated_scale, axis=0)
    gated_grad = gated_scale * scaled_grad - gated * gated_scale**3 * row_terms[:, None] / inner_all
    mixed_grad = gated_grad * gate_act
    gate_grad = (gated_grad * mixed * swish_slope(gate_raw)).astype(jnp.bfloat16)
    carry_entering = weighted_states(mixed_grad, jnp.exp(running), readers)
    leaving = relayed(carry_entering.reshape(state_shape), overall, "seq", True, 2)
    gating_grad = contract_first(normed, gate_grad)
    local_inner, state_act_grad, terms, (projection_grad, gating_grad) = backward_and_sums(
        (
            inner_x,
            writers,
            readers,
            deltas,
            running,
            across,
            flat_entering,
            skipping,
            mixed,
            mixed_grad,
            leaving.reshape(inner_here, statesize),
        ),
        (projection_grad.astype(jnp.bfloat16), gating_grad.astype(jnp.bfloat16)),
        3,
    )
    at_end = jnp.sum(terms[:, 2 * heads_here : 3 * heads_here], axis=0) + overall * jnp.sum(
        entering.astype(jnp.float32) * leaving.astype(jnp.float32), axis=(1, 2)
    )
    decays_grad = at_end[None, :] + lax.dot_general(
        causal, terms[:, :heads_here], (((0,), (0,)), ((), ())), precision=exact
    )
    deltas_grad = terms[:, heads_here : 2 * heads_here] + rates[None, :] * decays_grad
    skipgain_grad = jnp.sum(terms[:, 3 * heads_here :], axis=0)
    decaylog_grad = jnp.sum(deltas * decays_grad, axis=0) * rates
    step_full = deltas_grad * jax.nn.sigmoid(step_sum)
    stepbias_grad = jnp.sum(step_full, axis=0)
    step_grad = step_full.astype(jnp.bfloat16)
    state_act_grad = state_act_grad.astype(jnp.float32)
    local_inner = local_inner[None]
    state_act_grad = state_act_grad[None]
    act_grad = jnp.concatenate([local_inner, state_act_grad], axis=2)
    filtered_grad = act_grad * swish_slope(filtered)
    kernel_grad = jnp.stack(
        [
            jnp.sum(padded[:, tapindex : tapindex + tokens] * filtered_grad, axis=(0, 1))
            for tapindex in range(tapcount)
        ]
    )
    shifts_grad = jnp.sum(filtered_grad, axis=(0, 1))
    padded_grad = jnp.pad(
        kernel[0][None, None, :] * filtered_grad, ((0, 0), (0, tapcount - 1), (0, 0))
    )
    for tapindex in range(1, tapcount):
        padded_grad = padded_grad + jnp.pad(
            kernel[tapindex][None, None, :] * filtered_grad,
            ((0, 0), (tapindex, tapcount - 1 - tapindex), (0, 0)),
        )
    edge_back = passed_along(padded_grad[:, : tapcount - 1], "seq", -1)
    channel_grad = padded_grad[:, tapcount - 1 :] + jnp.pad(
        edge_back, ((0, 0), (tokens - tapcount + 1, 0), (0, 0))
    )
    inner_pre_grad = (
        channel_grad[:, :, :inner_here].reshape(rowcount, inner_here).astype(jnp.bfloat16)
    )
    state_pre_grad = channel_grad[:, :, inner_here:].reshape(rowcount, 2 * statesize)
    partial_in = (
        contract_last(gate_grad, gating)
        + contract_last(inner_pre_grad, feature)
        + contract_last(step_grad, timestep)
    )
    state_term = lax.dot_general(
        state_pre_grad, selective.astype(jnp.float32), (((1,), (1,)), ((), ())), precision=exact
    )
    mine = 2 * statesize // lax.axis_size("head")
    state_share = lax.dynamic_slice_in_dim(
        state_pre_grad, lax.axis_index("head") * mine, mine, 1
    )
    selective_grad = lax.dot_general(
        normed.astype(jnp.float32), state_share, (((0,), (0,)), ((), ())), precision=exact
    )
    statefilters_grad = kernel_grad[:, inner_here:]
    stateoffsets_grad = shifts_grad[inner_here:]
    feature_grad = contract_first(normed, inner_pre_grad)
    timestep_grad = contract_first(normed, step_grad)
    narrow = jnp.concatenate([selective_grad, timestep_grad], axis=1).astype(jnp.bfloat16)
    narrow = jnp.pad(narrow, ((0, 0), (0, -narrow.shape[1] % 128)))
    normed_grad, (feature_grad, narrow) = finished_sums(
        partial_in.astype(jnp.bfloat16),
        (
            feature_grad.astype(jnp.bfloat16),
            narrow,
        ),
        4,
    )
    normed_grad = normed_grad.astype(jnp.float32) + state_term
    prescale_grad = jnp.sum(normed_grad * flat_in * rowscale, axis=0)
    scaled_in = normed_grad * prescale[None, :]
    row_in = jnp.sum(scaled_in * flat_in, axis=1, keepdims=True)
    hidden_grad = (
        upstream.astype(jnp.float32)
        + rowscale * scaled_in
        - flat_in * rowscale**3 * row_in / modelwidth
    )
    hidden_grad = hidden_grad.reshape(seqcount, tokens, modelwidth)
    timestep_grad = narrow[:, mine : mine + heads_here]
    around = gathered(narrow.astype(jnp.bfloat16), "head", 5)[:, :, :mine]
    selective_grad = (
        around.transpose(1, 0, 2).reshape(narrow.shape[0], 2 * statesize).astype(jnp.float32)
    )
    small = (
        kernel_grad[:, :inner_here],
        statefilters_grad,
        shifts_grad[:inner_here],
        stateoffsets_grad,
        postscale_grad,
        prescale_grad,
        stepbias_grad,
        decaylog_grad,
        skipgain_grad,
    )
    packed = jnp.concatenate([part.reshape(-1) for part in small])
    packed = jnp.pad(packed, (0, -packed.shape[0] % 1024)).reshape(-1, 128)
    packed = jnp.sum(gathered(packed, "seq", 6), axis=0).reshape(-1)
    at, finished = 0, []
    for part in small:
        finished.append(packed[at : at + part.size].reshape(part.shape))
        at += part.size
    (
        filters_grad,
        statefilters_grad,
        offsets_grad,
        stateoffsets_grad,
        postscale_grad,
        prescale_grad,
        stepbias_grad,
        decaylog_grad,
        skipgain_grad,
    ) = finished
    owned = modelwidth // lax.axis_size("seq")
    prescale_grad = lax.dynamic_slice_in_dim(
        prescale_grad, lax.axis_index("seq") * owned, owned, 0
    )
    return (
        output,
        hidden_grad,
        prescale_grad,
        gating_grad,
        feature_grad,
        selective_grad,
        timestep_grad,
        filters_grad,
        statefilters_grad,
        offsets_grad,
        stateoffsets_grad,
        stepbias_grad,
        decaylog_grad,
        skipgain_grad,
        postscale_grad,
        projection_grad,
    )


def solution(mesh):
    placed = (
        P(None, "seq", None),
        P(),
        P(None, "head"),
        P(None, "head"),
        P(),
        P(None, "head"),
        P(None, "head"),
        P(),
        P("head"),
        P(),
        P("head"),
        P("head"),
        P("head"),
        P("head"),
        P(None, "head"),
        P(None, "seq", "head"),
    )
    return jax.shard_map(
        local,
        mesh=mesh,
        in_specs=placed,
        out_specs=(
            P(None, "seq", "head"),
            P(None, "seq", None),
            P("seq"),
            P("seq", "head"),
            P("seq", "head"),
            P("seq", None),
            P("seq", "head"),
            P(None, "head"),
            P(),
            P("head"),
            P(),
            P("head"),
            P("head"),
            P("head"),
            P("head"),
            P("seq", "head"),
        ),
        check_vma=False,
    )
```
